32 devices in a mesh: brick: 4 (over x, core), dom: 8 (over z, y).
Axes of the slice: x: 2, y: 2, z: 4, core: 2. Of those that a mesh axis runs over, the one named last changes fastest.
Arguments:
- velocity: bfloat16 [3, 27, 32768], P(None, None, ('brick', 'dom')), may hold values from -6 to 6
- adjoint: bfloat16 [3, 27, 32768], P(None, None, ('brick', 'dom')), may hold values from -6 to 6
- coupling: bfloat16 [27, 27], replicated, may hold values from -1.25 to 1.25
- jac_weight: float32 [32768], P(('brick', 'dom')), may hold values from 0.25 to 4
- owner: int32 [32768, 1], P(('brick', 'dom')), may hold values from 0 to 31; in each aligned block of 1024 rows (0 to 1023, 1024 to 2047, ...) at most 64 rows name the same one
- local_block: int32 [32768], P(('brick', 'dom')), may hold values from 0 to 4095
- offsets: int32 [128, 32768], P(None, ('brick', 'dom')), may hold values from 0 to 127
- margin: float32 [128, 32768], P(None, ('brick', 'dom')), may hold values from 0.002 to 0.02
- filtered: float32 [256, 512, 128], P('brick', 'dom'), may hold values from 0 to 1
Outputs:
- sensitivity: float32 [256, 512, 128], P('brick', 'dom')
- elem_density: float32 [32768], P(('brick', 'dom'))
The draws below stay inside these ranges and needn't reach their ends.
Inputs may be any that keep to these rules, and one draw needn't show every extreme that they name: Among the 1024 elements of one device at most 64 have the same owner, and exactly 64 for some owner.
All inputs are finite; a program needn't handle non-finite values.
Results may differ from the reference program's by a relative error of at most 0.0003.
Values sent between devices are 32-bit elements; how exact they have to be, the bound alone decides.
No kernel may reach another device: no remote copies, remote signals or barrier semaphores. Data moves between devices by JAX's collectives and lax.ppermute only.
A program may use at most 64 MiB of HBM per device.

```python
import math
import jax
import jax.numpy as jnp
import numpy as np
from jax import lax

BX = 64
BY = 64
GZ = 128
ELEM_DEV = 1024
SLOTS = 128
NDEV = 32
CAP = 64
NE = 32768
GX = 256
GY = 512
N_DOM = 8


def plant(array, key, low, largest):
    shape = array.shape
    index_at = [jax.random.randint(jax.random.fold_in(key, axis), (), 0, shape[axis]) for axis in range(len(shape))]
    array = array.at[tuple(index_at)].set(low)
    longest = shape.index(max(shape))
    index_at[longest] = (index_at[longest] + 1) % shape[longest]
    return array.at[tuple(index_at)].set(largest)


def shard_levels(key, dims, split, least, high):
    loudness, own = 1.0, jax.random.fold_in(key, 6)
    for axis_at, shards_of in split:
        steps = jnp.exp(jax.random.uniform(jax.random.fold_in(own, axis_at), (shards_of,), jnp.float32, least / len(split), high / len(split)))
        loudness = loudness * jnp.repeat(steps, dims[axis_at] // shards_of).reshape([-1 if axis == axis_at else 1 for axis in range(len(dims))])
    return loudness


def routed_block(key, own, number, rows, number_of, top, reach, lean):
    sequence = jax.random.permutation(key, number_of)
    crowded, common = load_shares(number_of, rows * top, reach, lean, True), load_shares(number_of, rows * top, reach, lean, False)
    places = jnp.arange(number_of)

    def named(sizes, turn):
        used = int((sizes > 0).sum())
        fixed = max(1, used // 4)
        moved = fixed + (places - fixed + turn * (used - fixed)) % max(1, number_of - fixed)
        return jnp.zeros((number_of,), jnp.int32).at[sequence[jnp.where(places < fixed, places, moved)]].set(jnp.asarray(sizes, jnp.int32))

    sizes = jnp.where(number % 4 == 0, named(crowded, number // 4), named(common, number - number // 4 - 1))
    mixed = jax.random.permutation(jax.random.fold_in(own, 3), number_of)
    source_of, sink = mixed[0:number_of // 2 * 2:2], mixed[1:number_of // 2 * 2:2]
    room = jnp.minimum(sizes[source_of] - 1, reach - sizes[sink]) // 2
    room = jnp.where((source_of == sequence[0]) | (sink == sequence[0]) | (sizes[sink] == 0), 0, jnp.maximum(room, 0))
    moved = jax.random.randint(jax.random.fold_in(own, 4), (number_of // 2,), 0, 1 << 20) % (room + 1)
    sizes = sizes.at[source_of].add(-moved).at[sink].add(moved)
    members = jnp.searchsorted(jnp.cumsum(sizes), jnp.arange(rows * top), side="right").astype(jnp.int32)
    table = members.reshape(top, rows).T
    table = table[jax.random.permutation(jax.random.fold_in(own, 1), rows)]
    turn = jax.random.randint(jax.random.fold_in(own, 2), (rows, 1), 0, top)
    return jnp.take_along_axis(table, (jnp.arange(top)[None, :] + turn) % top, axis=1)


def load_shares(number_of, total, reach, lean, full):
    loads = [(1 << 20) // math.isqrt(standing ** lean) + 1 for standing in range(1, number_of + 1)]
    largest = reach if full else min(reach, max(-(-total // number_of), total * loads[0] // sum(loads)))
    least = 1 if total - largest >= number_of - 1 else 0
    holding, rest = [largest] + [least] * (number_of - 1), total - largest - least * (number_of - 1)
    while rest > 0:
        movable = [i for i in range(1, number_of) if holding[i] < largest] or [i for i in range(1, number_of) if holding[i] < reach]
        whole, remaining = sum([loads[i] for i in movable]), rest
        for i in movable:
            addition = min(reach - holding[i], max(1, remaining * loads[i] // whole), rest)
            holding[i] = holding[i] + addition
            rest = rest - addition
    return np.array(holding)


def centred(key, extent, spread, most, cuts=(), held_as=jnp.bfloat16):
    factor_of = shard_levels(key, extent, cuts, -0.22, 0.18) if cuts else 1.0
    values = jax.random.normal(key, extent, jnp.float32) * spread * factor_of
    return jnp.minimum(jnp.maximum(values, -most), most).astype(held_as)


def setup_inputs(seed: int = 0) -> dict:
    streams_of = jax.random.split(jax.random.key(seed), 10)
    velocity = centred(streams_of[0], (3, 27, NE), 1.0, 6.0, ((2, 32),))
    adjoint = centred(streams_of[1], (3, 27, NE), 1.0, 6.0, ((2, 32),))
    coupling = centred(streams_of[2], (27, 27), 27 ** -0.5, 1.25)
    jac_weight = jnp.clip(jnp.exp(math.log(4.0) - 2.7725887 * jax.random.uniform(streams_of[3], (NE,), jnp.float32) ** shard_levels(streams_of[3], (NE,), ((0, 32),), -0.2, 0.2)), 0.25, 4.0)
    owner_keys = jax.random.split(jax.random.fold_in(streams_of[4], 1), NE // ELEM_DEV)
    owner_turns = jax.random.permutation(jax.random.fold_in(streams_of[4], 3), NE // ELEM_DEV)
    owner = jax.vmap(lambda own, number: routed_block(jax.random.fold_in(streams_of[4], 2), own, number, ELEM_DEV, NDEV, 1, CAP, 2))(owner_keys, owner_turns).reshape((NE, 1))
    local_block = plant(jax.random.randint(streams_of[5], (NE,), 0, BX * BY), jax.random.fold_in(streams_of[5], 1), 0, (BX * BY) - 1).astype(jnp.int32)
    offsets = plant(jax.random.randint(streams_of[6], (SLOTS, NE), 0, GZ), jax.random.fold_in(streams_of[6], 1), 0, GZ - 1).astype(jnp.int32)
    margin = jnp.clip(jnp.exp(math.log(0.02) - 2.30258502 * jax.random.uniform(streams_of[7], (SLOTS, NE), jnp.float32) ** shard_levels(streams_of[7], (SLOTS, NE), ((1, 32),), -0.2, 0.2)), 0.002, 0.02)
    filtered = jnp.clip(1.0 * jax.random.uniform(streams_of[8], (GX, GY, GZ), jnp.float32) ** shard_levels(streams_of[8], (GX, GY, GZ), ((0, 4), (1, 8)), -0.2, 0.2), 0.0, 1.0)
    return {"velocity": velocity, "adjoint": adjoint, "coupling": coupling, "jac_weight": jac_weight, "owner": owner, "local_block": local_block, "offsets": offsets, "margin": margin, "filtered": filtered}


sharpness = 8.0
threshold = 0.5
ramp_q = 0.1
radius_sq = 1.5
relax = 0.9


def project(field):
    base = jnp.tanh(sharpness * threshold)
    return (base + jnp.tanh(sharpness * (field - threshold))) / (base + jnp.tanh(sharpness * (1.0 - threshold)))


def projection_slope(field):
    base = jnp.tanh(sharpness * threshold)
    tangent = jnp.tanh(sharpness * (field - threshold))
    return sharpness * (1.0 - tangent * tangent) / (base + jnp.tanh(sharpness * (1.0 - threshold)))


def ramp_slope(density):
    return -ramp_q * (1.0 + ramp_q) / ((ramp_q + density) * (ramp_q + density))


def jacobi_sweep(field, source):
    padded = jnp.pad(field, 1)
    near = padded[2:, 1:-1, 1:-1] + padded[:-2, 1:-1, 1:-1]
    near = near + padded[1:-1, 2:, 1:-1] + padded[1:-1, :-2, 1:-1]
    near = near + padded[1:-1, 1:-1, 2:] + padded[1:-1, 1:-1, :-2]
    center = 1.0 + 6.0 * radius_sq
    return field + relax * (source - (center * field - radius_sq * near)) / center


def reference(velocity, adjoint, coupling, jac_weight, owner, local_block, offsets, margin, filtered):
    voxel_rows = project(filtered).reshape(GX * GY, GZ)
    mixed = jnp.einsum("ij,cje->cie", coupling.astype(jnp.float32), adjoint.astype(jnp.float32))
    products = jac_weight * jnp.sum(velocity.astype(jnp.float32) * mixed, axis=(0, 1))
    target = owner[:, 0]
    grid_x = (target // N_DOM) * BX + local_block // BY
    grid_y = (target % N_DOM) * BY + local_block % BY
    global_block = (grid_x * GY + grid_y).astype(jnp.int32)
    lanes = jnp.arange(GZ, dtype=jnp.int32)

    def partition(total, index):
        start = index * ELEM_DEV
        part_offsets = lax.dynamic_slice_in_dim(offsets, start, ELEM_DEV, 1)
        part_margin = lax.dynamic_slice_in_dim(margin, start, ELEM_DEV, 1)
        hits = part_offsets[:, :, None] == lanes[None, None, :]
        weights = jnp.sum(jnp.where(hits, part_margin[:, :, None], jnp.float32(0.0)), axis=0)
        blocks = lax.dynamic_slice_in_dim(global_block, start, ELEM_DEV, 0)
        density = jnp.sum(weights * voxel_rows[blocks], axis=1)
        terms = ramp_slope(density) * lax.dynamic_slice_in_dim(products, start, ELEM_DEV, 0)
        total = total.at[blocks].add(terms[:, None] * weights)
        return total, density

    total, density = lax.scan(partition, jnp.zeros((GX * GY, GZ), jnp.float32), jnp.arange(NDEV, dtype=jnp.int32))
    source = total.reshape(GX, GY, GZ) * projection_slope(filtered)
    first = jacobi_sweep(source, source)
    result = jacobi_sweep(first, source)
    return result, density.reshape(NE)
```

```python
import functools

import jax
import jax.numpy as jnp
from jax import lax
from jax.experimental import pallas as pl
from jax.experimental.pallas import tpu as pltpu
from jax.sharding import PartitionSpec as P

sharpness = 8.0
threshold = 0.5
ramp_q = 0.1
radius_sq = 1.5
relax = 0.9

VMEM_LIMIT = 48 * 1024 * 1024
BF16 = jnp.bfloat16
F32 = jnp.float32
I32 = jnp.int32


def params():
    return pltpu.CompilerParams(vmem_limit_bytes=VMEM_LIMIT)


def parts(x, count):
    found = []
    for _ in range(count - 1):
        head = x.astype(BF16)
        found.append(head)
        x = x - head.astype(F32)
    found.append(x.astype(BF16))
    return found


def dot_nt(a, b):
    return lax.dot_general(a, b, (((1,), (1,)), ((), ())), preferred_element_type=F32)


def dot_nn(a, b):
    return jnp.dot(a, b, preferred_element_type=F32)


def route_kernel(owner_ref, block_ref, jac_ref, vel_ref, adj_ref, coup_ref, meta_ref, rank_ref):
    devices, _, twice = meta_ref.shape
    capacity = twice // 2
    count = owner_ref.shape[1]
    group = 128
    owner = owner_ref[...]
    row_of = lax.broadcasted_iota(I32, (devices, group), 0)
    before = lax.broadcasted_iota(I32, (group, 2 * group), 0)
    after = lax.broadcasted_iota(I32, (group, 2 * group), 1)
    sums = ((before < after) | (after >= group)).astype(F32).astype(BF16)
    carry = jnp.zeros((devices, group), F32)
    matches, ranks = [], []
    for at in range(0, count, group):
        match = (row_of == owner[:, at : at + group]).astype(F32)
        totals = dot_nn(match.astype(BF16), sums)
        ranks.append(jnp.sum(match * (totals[:, :group] + carry), axis=0, keepdims=True))
        matches.append(match)
        carry = carry + totals[:, group:]
    rank = jnp.concatenate(ranks, axis=1).astype(I32)
    match = jnp.concatenate(matches, axis=1)
    rank_ref[...] = rank

    total = jnp.zeros((1, count), F32)
    for c in range(adj_ref.shape[0]):
        mixed = dot_nn(coup_ref[...], adj_ref[c])
        total = total + jnp.sum(vel_ref[c].astype(F32) * mixed, axis=0, keepdims=True)
    product = jac_ref[...] * total

    block = block_ref[...]
    pieces = [(block >> 6).astype(F32), (block & 63).astype(F32)]
    pieces += [p.astype(F32) for p in parts(product, 3)]
    at_rank = (lax.broadcasted_iota(I32, (capacity, count), 0) == rank).astype(F32).astype(BF16)
    left = jnp.concatenate([(match * p).astype(BF16) for p in pieces], axis=0)
    placed = dot_nt(left, at_rank)
    high, low, first, second, third = [
        placed[i * devices : (i + 1) * devices] for i in range(5)
    ]
    meta_ref[:, 0, :] = jnp.concatenate([high * 64.0 + low, first + (second + third)], axis=1)


def maps_kernel(rank_ref, owner_ref, off_ref, mar_ref, out_ref, map_ref):
    slots, depth = out_ref.shape
    entries, count = off_ref.shape
    group = 128
    sub = 8
    bands = depth // sub
    voxel = [lax.broadcasted_iota(I32, (sub, group), 0) + sub * k for k in range(bands)]

    for at in range(0, count, group):

        def step(chunk, totals, at=at):
            totals = list(totals)
            base = pl.multiple_of(chunk * sub, sub)
            offs = off_ref[pl.ds(base, sub), at : at + group]
            mars = mar_ref[pl.ds(base, sub), at : at + group]
            for s in range(sub):
                off = jnp.broadcast_to(offs[s : s + 1], (sub, group))
                mar = jnp.broadcast_to(mars[s : s + 1], (sub, group))
                for k in range(bands):
                    totals[k] = totals[k] + jnp.where(off == voxel[k], mar, 0.0)
            return tuple(totals)

        totals = lax.fori_loop(
            0, entries // sub, step, tuple(jnp.zeros((sub, group), F32) for _ in range(bands))
        )
        for k in range(bands):
            high, low = parts(totals[k], 2)
            map_ref[sub * k : sub * (k + 1), at : at + group] = high.astype(F32)
            map_ref[depth + sub * k : depth + sub * (k + 1), at : at + group] = low.astype(F32)


def place_kernel(capacity, rank_ref, owner_ref, off_ref, mar_ref, out_ref, map_ref):
    maps_kernel(rank_ref, owner_ref, off_ref, mar_ref, out_ref, map_ref)
    slots, depth = out_ref.shape
    count = off_ref.shape[1]
    place = owner_ref[...] * capacity + rank_ref[...]
    both = map_ref[...].astype(BF16)
    tile = 256
    for at in range(0, slots, tile):
        row_of = lax.broadcasted_iota(I32, (tile, count), 0) + at
        here = (row_of == place).astype(F32).astype(BF16)
        moved = dot_nt(here, both)
        out_ref[at : at + tile, :] = moved[:, :depth] + moved[:, depth:]


def gather_kernel(index_ref, field_ref, found_ref, slope_ref, proj_ref):
    rows = found_ref.shape[0]
    base = jnp.tanh(jnp.full((1, 1), sharpness * threshold, F32))
    ceiling = base + jnp.tanh(jnp.full((1, 1), sharpness * (1.0 - threshold), F32))
    tile = 256

    def project(i, _):
        at = pl.ds(pl.multiple_of(i * tile, tile), tile)
        tangent = jnp.tanh(sharpness * (field_ref[at, :] - threshold))
        proj_ref[at, :] = (base + tangent) / ceiling
        slope_ref[at, :] = sharpness * (1.0 - tangent * tangent) / ceiling
        return 0

    lax.fori_loop(0, field_ref.shape[0] // tile, project, 0)
    unroll = 16

    def fetch(i, _):
        for j in range(unroll):
            r = i * unroll + j
            found_ref[pl.ds(r, 1), :] = proj_ref[pl.ds(index_ref[r], 1), :]
        return 0

    lax.fori_loop(0, rows // unroll, fetch, 0)


def scatter_kernel(index_ref, prod_ref, weight_ref, found_ref, slope_ref, source_ref, ylow_ref, yhigh_ref, dens_ref, val_ref):
    rows, depth = weight_ref.shape
    width_x, width_y, _ = source_ref.shape
    ones = jnp.ones((2 * depth, depth), BF16)
    group = 128
    diagonal = lax.broadcasted_iota(I32, (group, depth), 0) == lax.broadcasted_iota(I32, (group, depth), 1)
    for at in range(0, rows, group):
        weight = weight_ref[at : at + group, :]
        high, low = parts(weight * found_ref[at : at + group, :], 2)
        density = dot_nn(jnp.concatenate([high, low], axis=1), ones)
        dens_ref[at // group : at // group + 1, :] = jnp.sum(
            jnp.where(diagonal, density, 0.0), axis=0, keepdims=True
        )
        shifted = ramp_q + density
        term = -ramp_q * (1.0 + ramp_q) / (shifted * shifted) * prod_ref[at : at + group, :]
        high, low = parts(term * weight, 2)
        val_ref[at : at + group, :depth] = high
        val_ref[at : at + group, depth:] = low
    planes = 4
    tile = planes * width_y

    def step(i, _):
        row_of = lax.broadcasted_iota(I32, (tile, rows), 0) + i * tile
        here = (row_of == index_ref[...]).astype(F32).astype(BF16)
        summed = dot_nn(here, val_ref[...])
        at = pl.ds(pl.multiple_of(i * tile, tile), tile)
        source = (summed[:, :depth] + summed[:, depth:]) * slope_ref[at, :]
        source_ref[pl.ds(i * planes, planes), :, :] = source.reshape(planes, width_y, depth)
        return 0

    lax.fori_loop(0, width_x // planes, step, 0)
    ylow_ref[0] = source_ref[:, 0, :]
    ylow_ref[1] = source_ref[:, 1, :]
    yhigh_ref[0] = source_ref[:, width_y - 2, :]
    yhigh_ref[1] = source_ref[:, width_y - 1, :]


def along_z(x):
    lane = lax.broadcasted_iota(I32, x.shape, x.ndim - 1)
    depth = x.shape[-1]
    up = jnp.where(lane == 0, 0.0, pltpu.roll(x, 1, x.ndim - 1))
    down = jnp.where(lane == depth - 1, 0.0, pltpu.roll(x, depth - 1, x.ndim - 1))
    return up + down


def along_y(x, low, high):
    row = lax.broadcasted_iota(I32, x.shape, 0)
    count = x.shape[0]
    up = jnp.where(row == 0, jnp.broadcast_to(low, x.shape), pltpu.roll(x, 1, 0))
    down = jnp.where(row == count - 1, jnp.broadcast_to(high, x.shape), pltpu.roll(x, count - 1, 0))
    return up + down


def sweep_kernel(inside_ref, source_ref, xlow_ref, xhigh_ref, ylow_ref, yhigh_ref, edge_low_ref, edge_high_ref, corner_low_ref, corner_high_ref, out_ref, near_ref, nlow_ref, nhigh_ref):
    width_x, width_y, depth = source_ref.shape
    center = 1.0 + 6.0 * radius_sq
    spread = relax * radius_sq / center
    scale = relax / center
    near_ref[0] = inside_ref[0] * (
        along_z(xlow_ref[1])
        + along_y(xlow_ref[1], corner_low_ref[0:1], corner_low_ref[1:2])
        + xlow_ref[0]
        + source_ref[0]
    )
    near_ref[width_x + 1] = inside_ref[1] * (
        along_z(xhigh_ref[0])
        + along_y(xhigh_ref[0], corner_high_ref[0:1], corner_high_ref[1:2])
        + xhigh_ref[1]
        + source_ref[width_x - 1]
    )
    nlow_ref[...] = inside_ref[2] * (
        along_z(ylow_ref[1])
        + along_y(ylow_ref[1], corner_low_ref[0:1], corner_high_ref[0:1])
        + ylow_ref[0]
        + edge_low_ref[...]
    )
    nhigh_ref[...] = inside_ref[3] * (
        along_z(yhigh_ref[0])
        + along_y(yhigh_ref[0], corner_low_ref[1:2], corner_high_ref[1:2])
        + yhigh_ref[1]
        + edge_high_ref[...]
    )

    def neighbours(x, here, below, above, low, high):
        return along_z(here) + along_y(here, low, high) + below + above

    def first(x, _):
        near_ref[x + 1] = neighbours(
            x,
            source_ref[x],
            source_ref[x - 1],
            source_ref[x + 1],
            ylow_ref[1, pl.ds(x, 1), :],
            yhigh_ref[0, pl.ds(x, 1), :],
        )
        return 0

    near_ref[1] = neighbours(
        0, source_ref[0], xlow_ref[1], source_ref[1], ylow_ref[1, 0:1, :], yhigh_ref[0, 0:1, :]
    )
    lax.fori_loop(1, width_x - 1, first, 0)
    near_ref[width_x] = neighbours(
        width_x - 1,
        source_ref[width_x - 1],
        source_ref[width_x - 2],
        xhigh_ref[0],
        ylow_ref[1, width_x - 1 : width_x, :],
        yhigh_ref[0, width_x - 1 : width_x, :],
    )
    own = 1.0 - relax
    first_own = own + scale

    def second(x, _):
        here = near_ref[x + 1]
        again = neighbours(
            x,
            here,
            near_ref[x],
            near_ref[x + 2],
            nlow_ref[pl.ds(x, 1), :],
            nhigh_ref[pl.ds(x, 1), :],
        )
        out_ref[x] = (
            (own * first_own + scale) * source_ref[x]
            + (own * spread + spread * first_own) * here
            + (spread * spread) * again
        )
        return 0

    lax.fori_loop(0, width_x, second, 0)


def reply_kernel(rank_ref, owner_ref, reply_ref, out_ref):
    devices, capacity = reply_ref.shape
    count = rank_ref.shape[1]
    at_rank = (lax.broadcasted_iota(I32, (capacity, count), 0) == rank_ref[...]).astype(F32).astype(BF16)
    total = jnp.zeros((devices, count), F32)
    for piece in parts(reply_ref[...], 3):
        total = total + dot_nn(piece, at_rank)
    match = lax.broadcasted_iota(I32, (devices, count), 0) == owner_ref[...]
    out_ref[...] = jnp.sum(jnp.where(match, total, 0.0), axis=0, keepdims=True)


def shift(x, axis, up):
    count = lax.axis_size(axis)
    pairs = [(i, i + 1) if up else (i + 1, i) for i in range(count - 1)]
    return lax.ppermute(x, axis, pairs)


def body(velocity, adjoint, coupling, jac_weight, owner, local_block, offsets, margin, filtered):
    both = ("brick", "dom")
    brick_count = lax.axis_size("brick")
    dom_count = lax.axis_size("dom")
    devices = brick_count * dom_count
    count = owner.shape[0]
    width_x, width_y, depth = filtered.shape
    capacity = max(2, 2 * count // devices)
    slots = devices * capacity
    shape = jax.ShapeDtypeStruct

    owner_row = owner.reshape(1, count)
    meta, rank = pl.pallas_call(
        route_kernel,
        out_shape=(shape((devices, 1, 2 * capacity), F32), shape((1, count), I32)),
        compiler_params=params(),
        name="route",
    )(
        owner_row,
        local_block.reshape(1, count),
        jac_weight.reshape(1, count),
        velocity,
        adjoint,
        coupling,
    )
    meta = lax.all_to_all(meta, both, split_axis=0, concat_axis=0, tiled=True)
    outgoing = pl.pallas_call(
        functools.partial(place_kernel, capacity),
        out_shape=shape((slots, depth), F32),
        scratch_shapes=[pltpu.VMEM((2 * depth, count), F32)],
        compiler_params=params(),
        name="maps",
    )(rank, owner_row, offsets, margin)
    weights = lax.all_to_all(
        outgoing.reshape(devices, capacity, depth), both, split_axis=0, concat_axis=0, tiled=True
    ).reshape(slots, depth)

    index = meta[:, 0, :capacity].reshape(slots).astype(I32)
    prods = jnp.broadcast_to(meta[:, 0, capacity:].reshape(slots, 1), (slots, depth))
    vmem = pl.BlockSpec(memory_space=pltpu.VMEM)
    smem = pl.BlockSpec(memory_space=pltpu.SMEM)
    found, slope = pl.pallas_call(
        gather_kernel,
        out_shape=(shape((slots, depth), F32), shape((width_x * width_y, depth), F32)),
        in_specs=[smem, vmem],
        out_specs=(vmem, vmem),
        scratch_shapes=[pltpu.VMEM((width_x * width_y, depth), F32)],
        compiler_params=params(),
        name="gather",
    )(index, filtered.reshape(width_x * width_y, depth))
    source, yfirst, ylast, density = pl.pallas_call(
        scatter_kernel,
        out_shape=(
            shape((width_x, width_y, depth), F32),
            shape((2, width_x, depth), F32),
            shape((2, width_x, depth), F32),
            shape((slots // 128, 128), F32),
        ),
        scratch_shapes=[pltpu.VMEM((slots, 2 * depth), BF16)],
        compiler_params=params(),
        name="scatter",
    )(index.reshape(1, slots), prods, weights, found, slope)

    reply = lax.all_to_all(
        density.reshape(devices, 1, capacity), both, split_axis=0, concat_axis=0, tiled=True
    )
    element_density = pl.pallas_call(
        reply_kernel,
        out_shape=shape((1, count), F32),
        compiler_params=params(),
        name="reply",
    )(rank, owner_row, reply.reshape(devices, capacity))

    ylow = shift(ylast, "dom", True)
    yhigh = shift(yfirst, "dom", False)
    top = jnp.concatenate(
        [source[width_x - 2], source[width_x - 1], ylow[1, width_x - 1 :], yhigh[0, width_x - 1 :], jnp.zeros((6, depth), F32)]
    )
    bottom = jnp.concatenate(
        [source[0], source[1], ylow[1, :1], yhigh[0, :1], jnp.zeros((6, depth), F32)]
    )
    from_low = shift(top, "brick", True)
    from_high = shift(bottom, "brick", False)
    brick, dom = lax.axis_index("brick"), lax.axis_index("dom")
    inside = jnp.stack([brick > 0, brick < brick_count - 1, dom > 0, dom < dom_count - 1]).astype(F32)
    result = pl.pallas_call(
        sweep_kernel,
        out_shape=shape((width_x, width_y, depth), F32),
        in_specs=[smem] + [vmem] * 9,
        out_specs=vmem,
        scratch_shapes=[
            pltpu.VMEM((width_x + 2, width_y, depth), F32),
            pltpu.VMEM((width_x, depth), F32),
            pltpu.VMEM((width_x, depth), F32),
        ],
        compiler_params=params(),
        name="sweep",
    )(
        inside,
        source,
        from_low[: 2 * width_y].reshape(2, width_y, depth),
        from_high[: 2 * width_y].reshape(2, width_y, depth),
        ylow,
        yhigh,
        yfirst[0],
        ylast[1],
        from_low[2 * width_y : 2 * width_y + 8],
        from_high[2 * width_y : 2 * width_y + 8],
    )
    return (result, element_density.reshape(count))


def solution(mesh):
    return jax.shard_map(
        body,
        mesh=mesh,
        in_specs=(
            P(None, None, ("brick", "dom")),
            P(None, None, ("brick", "dom")),
            P(),
            P(("brick", "dom")),
            P(("brick", "dom"), None),
            P(("brick", "dom")),
            P(None, ("brick", "dom")),
            P(None, ("brick", "dom")),
            P("brick", "dom", None),
        ),
        out_specs=(P("brick", "dom", None), P(("brick", "dom"))),
        check_vma=False,
    )
```

```python
import functools

import jax
import jax.numpy as jnp
from jax import lax
from jax.experimental import pallas as pl
from jax.experimental.pallas import tpu as pltpu
from jax.sharding import PartitionSpec as P

sharpness = 8.0
threshold = 0.5
ramp_q = 0.1
radius_sq = 1.5
relax = 0.9

VMEM_LIMIT = 32 * 1024 * 1024
VMEM_WHOLE = 60 * 1024 * 1024
BF16 = jnp.bfloat16
F32 = jnp.float32
I32 = jnp.int32


def params(limit=VMEM_LIMIT):
    return pltpu.CompilerParams(vmem_limit_bytes=limit)


def parts(x, count):
    found = []
    for _ in range(count - 1):
        head = x.astype(BF16)
        found.append(head)
        x = x - head.astype(F32)
    found.append(x.astype(BF16))
    return found


def dot_nt(a, b):
    return lax.dot_general(a, b, (((1,), (1,)), ((), ())), preferred_element_type=F32)


def dot_nn(a, b):
    return jnp.dot(a, b, preferred_element_type=F32)


def fetch(sources, targets, sems):
    copies = [
        pltpu.make_async_copy(source, target, sems.at[i])
        for i, (source, target) in enumerate(zip(sources, targets))
    ]
    for copy in copies:
        copy.start()
    return copies


def send_kernel(owner_at, block_at, jac_at, vel_at, adj_at, coup_at, off_at, mar_at, out_ref, rank_ref, owner_ref, block_ref, jac_ref, vel_ref, adj_ref, coup_ref, off_ref, mar_ref, high_ref, low_ref, first_ref, second_ref, hist_ref, map_ref, sems, *, devices, capacity):
    copies = fetch(
        [off_at, mar_at, owner_at, block_at, jac_at, vel_at, adj_at, coup_at],
        [off_ref, mar_ref, owner_ref, block_ref, jac_ref, vel_ref, adj_ref, coup_ref],
        sems,
    )
    slots, depth = out_ref.shape
    stride = slots // devices
    entries, count = off_ref.shape
    group = 128

    row_of = lax.broadcasted_iota(I32, (devices, group), 0)
    before = lax.broadcasted_iota(I32, (group, 2 * group), 0)
    after = lax.broadcasted_iota(I32, (group, 2 * group), 1)
    sums = ((before < after) | (after >= group)).astype(F32).astype(BF16)
    for copy in copies[2:]:
        copy.wait()
    owner = owner_ref[...]
    carry = jnp.zeros((devices, group), F32)
    matches, ranks = [], []
    for at in range(0, count, group):
        match = (row_of == owner[:, at : at + group]).astype(F32)
        totals = dot_nn(match.astype(BF16), sums)
        ranks.append(jnp.sum(match * (totals[:, :group] + carry), axis=0, keepdims=True))
        matches.append(match)
        carry = carry + totals[:, group:]
    rank = jnp.concatenate(ranks, axis=1).astype(I32)
    match = jnp.concatenate(matches, axis=1)
    rank_ref[...] = rank

    total = jnp.zeros((1, count), F32)
    for c in range(adj_ref.shape[0]):
        mixed = dot_nn(coup_ref[...], adj_ref[c])
        total = total + jnp.sum(vel_ref[c].astype(F32) * mixed, axis=0, keepdims=True)
    product = jac_ref[...] * total

    block = block_ref[...]
    pieces = [(block >> 6).astype(F32), (block & 63).astype(F32)]
    pieces += [p.astype(F32) for p in parts(product, 3)]
    at_rank = (lax.broadcasted_iota(I32, (capacity, count), 0) == rank).astype(F32).astype(BF16)
    left = jnp.concatenate([(match * p).astype(BF16) for p in pieces], axis=0)
    placed = dot_nt(left, at_rank)
    high, low, first, second, third = [
        placed[i * devices : (i + 1) * devices] for i in range(5)
    ]
    meta = [high * 64.0 + low, first + (second + third)]
    if 2 * capacity < depth:
        meta.append(jnp.zeros((devices, depth - 2 * capacity), F32))
    meta = jnp.concatenate(meta, axis=1)

    sets = count // group
    lows = group // sets
    highs = depth // lows
    for copy in copies[:2]:
        copy.wait()
    for b in range(sets):
        off = off_ref[:, b * group : (b + 1) * group].T
        mar = mar_ref[:, b * group : (b + 1) * group].T
        first = mar.astype(BF16).astype(F32)
        high_ref[b] = off // lows
        low_ref[b] = off % lows
        first_ref[b] = first
        second_ref[b] = mar - first

    high_of = lax.broadcasted_iota(I32, (highs, entries), 0)
    low_of = lax.broadcasted_iota(I32, (lows, entries), 0)
    set_of = lax.broadcasted_iota(I32, (highs, group), 1) // lows
    unroll = 32

    def step(i, _):
        for j in range(unroll):
            g = i * unroll + j
            left, right = [], []
            for b in range(sets):
                here = jnp.broadcast_to(high_ref[b, pl.ds(g, 1), :], (highs, entries)) == high_of
                for part_ref in (first_ref, second_ref):
                    part = jnp.broadcast_to(part_ref[b, pl.ds(g, 1), :], (highs, entries))
                    left.append(jnp.where(here, part, 0.0))
                right.append(
                    (jnp.broadcast_to(low_ref[b, pl.ds(g, 1), :], (lows, entries)) == low_of).astype(F32)
                )
            both = dot_nt(
                jnp.concatenate(left, axis=0).astype(BF16),
                jnp.concatenate(right, axis=0).astype(BF16),
            )
            hist = jnp.zeros((highs, group), F32)
            for b in range(sets):
                at = 2 * highs * b
                total = both[at : at + highs] + both[at + highs : at + 2 * highs]
                hist = jnp.where(set_of == b, total, hist)
            hist_ref[pl.ds(pl.multiple_of(g * highs, highs), highs), :] = hist
        return 0

    lax.fori_loop(0, group // unroll, step, 0)
    for h in range(highs):
        turned = hist_ref[pl.ds(h, group, stride=highs), :].T
        first = turned.astype(BF16)
        second = (turned - first.astype(F32)).astype(BF16)
        for b in range(sets):
            columns = slice(b * group, (b + 1) * group)
            map_ref[h * lows : (h + 1) * lows, columns] = first[b * lows : (b + 1) * lows]
            map_ref[depth + h * lows : depth + (h + 1) * lows, columns] = second[b * lows : (b + 1) * lows]

    place = owner * stride + rank
    tile = slots // 4
    for at in range(0, slots, tile):
        row_of = lax.broadcasted_iota(I32, (tile, count), 0) + at
        here = (row_of == place).astype(F32).astype(BF16)
        moved = dot_nt(here, map_ref[...])
        out_ref[at : at + tile, :] = moved[:, :depth] + moved[:, depth:]
    for d in range(devices):
        row = d * stride + capacity
        out_ref[row : row + 1, :] = meta[d : d + 1, :]


def constants():
    base = jnp.tanh(jnp.full((1, 1), sharpness * threshold, F32))
    return base, base + jnp.tanh(jnp.full((1, 1), sharpness * (1.0 - threshold), F32))


def owner_kernel(got_ref, field_ref, source_ref, ylow_ref, yhigh_ref, dens_ref, meta_ref, block_ref, found_ref, val_ref, y_ref, number_ref, sem, *, capacity):
    devices = dens_ref.shape[0]
    stride = got_ref.shape[0] // devices
    depth = got_ref.shape[1]
    rows = devices * capacity
    width_x, width_y, _ = source_ref.shape
    group = 128

    for d in range(devices):
        row = d * stride + capacity
        meta_ref[d : d + 1, :] = got_ref[row : row + 1, :]
    meta = meta_ref[...]
    block_ref[...] = meta.astype(I32)
    copy = pltpu.make_async_copy(block_ref, number_ref, sem)
    copy.start()
    prods = meta.T
    joined = group // capacity
    index = [
        jnp.concatenate(
            [block_ref[d + j : d + j + 1, :capacity] for j in range(joined)], axis=1
        )
        for d in range(0, devices, joined)
    ]
    y_of = lax.broadcasted_iota(I32, (width_y, group), 0)
    for k, part in enumerate(index):
        y_ref[:, k * group : (k + 1) * group] = (y_of == part % width_y).astype(F32).astype(BF16)
    x_row = jnp.concatenate(index, axis=1) // width_y
    copy.wait()

    def look(d, _):
        for r in range(capacity):
            found_ref[pl.ds(d * capacity + r, 1), :] = field_ref[pl.ds(number_ref[d, r], 1), :]
        return 0

    lax.fori_loop(0, devices, look, 0)

    base, ceiling = constants()
    inverse = 1.0 / ceiling
    for d in range(devices):
        at = slice(d * capacity, (d + 1) * capacity)
        tangent = jnp.tanh(sharpness * (found_ref[at, :] - threshold))
        weight = got_ref[d * stride : d * stride + capacity, :]
        high, low = parts(weight * ((base + tangent) * inverse), 2)
        val_ref[at, :depth] = high
        val_ref[at, depth:] = low
    found_ref[...] = dot_nn(val_ref[...], jnp.ones((2 * depth, depth), BF16))
    diagonal = lax.broadcasted_iota(I32, (capacity, depth), 0) == lax.broadcasted_iota(I32, (capacity, depth), 1)
    for d in range(devices):
        at = slice(d * capacity, (d + 1) * capacity)
        density = found_ref[at, :]
        dens_ref[d, :, :] = jnp.sum(jnp.where(diagonal, density, 0.0), axis=0, keepdims=True)[:, :capacity]
        shifted = ramp_q + density
        term = -ramp_q * (1.0 + ramp_q) / (shifted * shifted) * prods[capacity : 2 * capacity, d : d + 1]
        high, low = parts(term * got_ref[d * stride : d * stride + capacity, :], 2)
        val_ref[at, :depth] = high
        val_ref[at, depth:] = low

    planes = 16
    tile = planes * width_y

    def step(i, _):
        here = []
        for j in range(planes):
            at_x = (x_row == i * planes + j).astype(F32)
            here.append(y_ref[...] * jnp.broadcast_to(at_x, (width_y, rows)).astype(BF16))
        summed = dot_nn(jnp.concatenate(here, axis=0), val_ref[...])
        at = pl.ds(pl.multiple_of(i * tile, tile), tile)
        tangent = jnp.tanh(sharpness * (field_ref[at, :] - threshold))
        slope = sharpness * inverse * (1.0 - tangent * tangent)
        source = (summed[:, :depth] + summed[:, depth:]) * slope
        source_ref[pl.ds(i * planes, planes), :, :] = source.reshape(planes, width_y, depth)
        return 0

    lax.fori_loop(0, width_x // planes, step, 0)
    ylow_ref[0] = source_ref[:, 0, :]
    ylow_ref[1] = source_ref[:, 1, :]
    yhigh_ref[0] = source_ref[:, width_y - 2, :]
    yhigh_ref[1] = source_ref[:, width_y - 1, :]


def along_z(x):
    lane = lax.broadcasted_iota(I32, x.shape, x.ndim - 1)
    depth = x.shape[-1]
    up = jnp.where(lane == 0, 0.0, pltpu.roll(x, 1, x.ndim - 1))
    down = jnp.where(lane == depth - 1, 0.0, pltpu.roll(x, depth - 1, x.ndim - 1))
    return up + down


def along_rows(x, low, high):
    row = lax.broadcasted_iota(I32, x.shape, 0)
    count = x.shape[0]
    up = jnp.where(row == 0, jnp.broadcast_to(low, x.shape), pltpu.roll(x, 1, 0))
    down = jnp.where(row == count - 1, jnp.broadcast_to(high, x.shape), pltpu.roll(x, count - 1, 0))
    return up + down


def sweep_kernel(inside_ref, source_ref, xlow_ref, xhigh_ref, ylow_ref, yhigh_ref, edge_low_ref, edge_high_ref, corner_low_ref, corner_high_ref, out_at, wide_ref, near_ref, out_ref, sems):
    width_x, width_y, depth = source_ref.shape
    pad = 8
    inner = slice(pad, pad + width_y)
    center = 1.0 + 6.0 * radius_sq
    spread = relax * radius_sq / center
    scale = relax / center
    own = 1.0 - relax
    first_own = own + scale
    planes = 8

    def widen(i, _):
        at = i * planes
        wide_ref[pl.ds(at + 2, planes), inner, :] = source_ref[pl.ds(at, planes)]
        return 0

    lax.fori_loop(0, width_x // planes, widen, 0)
    wide_ref[0:2, inner, :] = xlow_ref[...]
    wide_ref[width_x + 2 : width_x + 4, inner, :] = xhigh_ref[...]
    wide_ref[2 : width_x + 2, pad - 1, :] = ylow_ref[1]
    wide_ref[2 : width_x + 2, pad + width_y, :] = yhigh_ref[0]
    wide_ref[1, pad - 1 : pad, :] = corner_low_ref[0:1]
    wide_ref[1, pad + width_y : pad + width_y + 1, :] = corner_low_ref[1:2]
    wide_ref[width_x + 2, pad - 1 : pad, :] = corner_high_ref[0:1]
    wide_ref[width_x + 2, pad + width_y : pad + width_y + 1, :] = corner_high_ref[1:2]

    def neighbours(ref, at):
        return (
            along_z(ref[at, inner, :])
            + (ref[at, pad - 1 : pad + width_y - 1, :] + ref[at, pad + 1 : pad + width_y + 1, :])
            + (ref[at - 1, inner, :] + ref[at + 1, inner, :])
        )

    group = 6

    def first(i, _):
        for j in range(group):
            at = i * group + j
            near_ref[at, inner, :] = neighbours(wide_ref, at + 1)
        return 0

    total = width_x + 2
    while total % group:
        group -= 1
    lax.fori_loop(0, total // group, first, 0)
    near_ref[0, inner, :] = near_ref[0, inner, :] * inside_ref[0]
    near_ref[width_x + 1, inner, :] = near_ref[width_x + 1, inner, :] * inside_ref[1]
    near_ref[1 : width_x + 1, pad - 1, :] = inside_ref[2] * (
        along_z(ylow_ref[1])
        + along_rows(ylow_ref[1], corner_low_ref[0:1], corner_high_ref[0:1])
        + ylow_ref[0]
        + edge_low_ref[...]
    )
    near_ref[1 : width_x + 1, pad + width_y, :] = inside_ref[3] * (
        along_z(yhigh_ref[0])
        + along_rows(yhigh_ref[0], corner_low_ref[1:2], corner_high_ref[1:2])
        + yhigh_ref[1]
        + edge_high_ref[...]
    )

    def second(i, _):
        for j in range(planes):
            x = i * planes + j
            out_ref[x] = (
                (own * first_own + scale) * source_ref[x]
                + (own * spread + spread * first_own) * near_ref[x + 1, inner, :]
                + (spread * spread) * neighbours(near_ref, x + 1)
            )
        at = pl.ds(i * planes, planes)
        pltpu.make_async_copy(out_ref.at[at], out_at.at[at], sems.at[i]).start()
        return 0

    lax.fori_loop(0, width_x // planes, second, 0)

    def settle(i, _):
        at = pl.ds(i * planes, planes)
        pltpu.make_async_copy(out_ref.at[at], out_at.at[at], sems.at[i]).wait()
        return 0

    lax.fori_loop(0, width_x // planes, settle, 0)


def reply_kernel(rank_ref, owner_ref, reply_ref, out_ref):
    devices, capacity = reply_ref.shape
    count = rank_ref.shape[1]
    at_rank = (lax.broadcasted_iota(I32, (capacity, count), 0) == rank_ref[...]).astype(F32).astype(BF16)
    total = jnp.zeros((devices, count), F32)
    for piece in parts(reply_ref[...], 3):
        total = total + dot_nn(piece, at_rank)
    match = lax.broadcasted_iota(I32, (devices, count), 0) == owner_ref[...]
    out_ref[...] = jnp.sum(jnp.where(match, total, 0.0), axis=0, keepdims=True)


def shift(x, axis, up):
    count = lax.axis_size(axis)
    pairs = [(i, i + 1) if up else (i + 1, i) for i in range(count - 1)]
    return lax.ppermute(x, axis, pairs)


def body(velocity, adjoint, coupling, jac_weight, owner, local_block, offsets, margin, filtered):
    both = ("brick", "dom")
    brick_count = lax.axis_size("brick")
    dom_count = lax.axis_size("dom")
    devices = brick_count * dom_count
    count = owner.shape[0]
    width_x, width_y, depth = filtered.shape
    capacity = max(2, 2 * count // devices)
    slots = devices * capacity
    shape = jax.ShapeDtypeStruct
    vmem = pl.BlockSpec(memory_space=pltpu.VMEM)
    smem = pl.BlockSpec(memory_space=pltpu.SMEM)
    hbm = pl.BlockSpec(memory_space=pltpu.HBM)

    owner_row = owner.reshape(1, count)
    stride = capacity + -(-2 * capacity // depth)
    lanes = 128
    turned = (count // lanes, lanes, offsets.shape[0])
    outgoing, rank = pl.pallas_call(
        functools.partial(send_kernel, devices=devices, capacity=capacity),
        out_shape=(shape((devices * stride, depth), F32), shape((1, count), I32)),
        in_specs=[hbm] * 8,
        out_specs=(vmem, vmem),
        scratch_shapes=[
            pltpu.VMEM((1, count), I32),
            pltpu.VMEM((1, count), I32),
            pltpu.VMEM((1, count), F32),
            pltpu.VMEM(velocity.shape, BF16),
            pltpu.VMEM(adjoint.shape, BF16),
            pltpu.VMEM(coupling.shape, BF16),
            pltpu.VMEM(offsets.shape, I32),
            pltpu.VMEM(margin.shape, F32),
            pltpu.VMEM(turned, I32),
            pltpu.VMEM(turned, I32),
            pltpu.VMEM(turned, F32),
            pltpu.VMEM(turned, F32),
            pltpu.VMEM((count * depth // lanes, lanes), F32),
            pltpu.VMEM((2 * depth, count), BF16),
            pltpu.SemaphoreType.DMA((8,)),
        ],
        compiler_params=params(VMEM_WHOLE),
        name="send",
    )(
        owner_row,
        local_block.reshape(1, count),
        jac_weight.reshape(1, count),
        velocity,
        adjoint,
        coupling,
        offsets,
        margin,
    )
    got = lax.all_to_all(
        outgoing.reshape(devices, 1, stride * depth), both, split_axis=0, concat_axis=0, tiled=True
    ).reshape(devices * stride, depth)
    source, yfirst, ylast, density = pl.pallas_call(
        functools.partial(owner_kernel, capacity=capacity),
        out_shape=(
            shape((width_x, width_y, depth), F32),
            shape((2, width_x, depth), F32),
            shape((2, width_x, depth), F32),
            shape((devices, 1, capacity), F32),
        ),
        scratch_shapes=[
            pltpu.VMEM((devices, depth), F32),
            pltpu.VMEM((devices, depth), I32),
            pltpu.VMEM((slots, depth), F32),
            pltpu.VMEM((slots, 2 * depth), BF16),
            pltpu.VMEM((width_y, slots), BF16),
            pltpu.SMEM((devices, depth), I32),
            pltpu.SemaphoreType.DMA,
        ],
        compiler_params=params(),
        name="owners",
    )(got, filtered.reshape(width_x * width_y, depth))

    reply = lax.all_to_all(
        density, both, split_axis=0, concat_axis=0, tiled=True
    )
    element_density = pl.pallas_call(
        reply_kernel,
        out_shape=shape((1, count), F32),
        compiler_params=params(),
        name="reply",
    )(rank, owner_row, reply.reshape(devices, capacity))

    ylow = shift(ylast, "dom", True)
    yhigh = shift(yfirst, "dom", False)
    top = jnp.concatenate(
        [source[width_x - 2], source[width_x - 1], ylow[1, width_x - 1 :], yhigh[0, width_x - 1 :], jnp.zeros((6, depth), F32)]
    )
    bottom = jnp.concatenate(
        [source[0], source[1], ylow[1, :1], yhigh[0, :1], jnp.zeros((6, depth), F32)]
    )
    from_low = shift(top, "brick", True)
    from_high = shift(bottom, "brick", False)
    brick, dom = lax.axis_index("brick"), lax.axis_index("dom")
    inside = jnp.stack([brick > 0, brick < brick_count - 1, dom > 0, dom < dom_count - 1]).astype(F32)
    result = pl.pallas_call(
        sweep_kernel,
        out_shape=shape((width_x, width_y, depth), F32),
        in_specs=[smem] + [vmem] * 9,
        out_specs=hbm,
        scratch_shapes=[
            pltpu.VMEM((width_x + 4, width_y + 16, depth), F32),
            pltpu.VMEM((width_x + 2, width_y + 16, depth), F32),
            pltpu.VMEM((width_x, width_y, depth), F32),
            pltpu.SemaphoreType.DMA((width_x // 8,)),
        ],
        compiler_params=params(),
        name="sweep",
    )(
        inside,
        source,
        from_low[: 2 * width_y].reshape(2, width_y, depth),
        from_high[: 2 * width_y].reshape(2, width_y, depth),
        ylow,
        yhigh,
        yfirst[0],
        ylast[1],
        from_low[2 * width_y : 2 * width_y + 8],
        from_high[2 * width_y : 2 * width_y + 8],
    )
    return (result, element_density.reshape(count))


def solution(mesh):
    return jax.shard_map(
        body,
        mesh=mesh,
        in_specs=(
            P(None, None, ("brick", "dom")),
            P(None, None, ("brick", "dom")),
            P(),
            P(("brick", "dom")),
            P(("brick", "dom"), None),
            P(("brick", "dom")),
            P(None, ("brick", "dom")),
            P(None, ("brick", "dom")),
            P("brick", "dom", None),
        ),
        out_specs=(P("brick", "dom", None), P(("brick", "dom"))),
        check_vma=False,
    )
```

```python
import functools

import jax
import jax.numpy as jnp
from jax import lax
from jax.experimental import pallas as pl
from jax.experimental.pallas import tpu as pltpu
from jax.sharding import PartitionSpec as P

sharpness = 8.0
threshold = 0.5
ramp_q = 0.1
radius_sq = 1.5
relax = 0.9

VMEM_LIMIT = 32 * 1024 * 1024
VMEM_WHOLE = 60 * 1024 * 1024
BF16 = jnp.bfloat16
F32 = jnp.float32
I32 = jnp.int32


def params(limit=VMEM_LIMIT):
    return pltpu.CompilerParams(vmem_limit_bytes=limit)


def parts(x, count):
    found = []
    for _ in range(count - 1):
        head = x.astype(BF16)
        found.append(head)
        x = x - head.astype(F32)
    found.append(x.astype(BF16))
    return found


def dot_nt(a, b):
    return lax.dot_general(a, b, (((1,), (1,)), ((), ())), preferred_element_type=F32)


def dot_nn(a, b):
    return jnp.dot(a, b, preferred_element_type=F32)


def fetch(sources, targets, sems):
    copies = [
        pltpu.make_async_copy(source, target, sems.at[i])
        for i, (source, target) in enumerate(zip(sources, targets))
    ]
    for copy in copies:
        copy.start()
    return copies


def send_kernel(owner_at, block_at, jac_at, vel_at, adj_at, coup_at, off_at, mar_at, out_at, rank_ref, owner_ref, block_ref, jac_ref, vel_ref, adj_ref, coup_ref, off_ref, mar_ref, high_ref, low_ref, first_ref, second_ref, hist_ref, map_ref, out_ref, sems, *, devices, capacity):
    copies = fetch(
        [owner_at, block_at, jac_at, vel_at, adj_at, coup_at, off_at, mar_at],
        [owner_ref, block_ref, jac_ref, vel_ref, adj_ref, coup_ref, off_ref, mar_ref],
        sems,
    )
    slots, depth = out_ref.shape
    stride = slots // devices
    entries, count = off_ref.shape
    group = 128

    row_of = lax.broadcasted_iota(I32, (devices, group), 0)
    before = lax.broadcasted_iota(I32, (group, 2 * group), 0)
    after = lax.broadcasted_iota(I32, (group, 2 * group), 1)
    sums = ((before < after) | (after >= group)).astype(F32).astype(BF16)
    for copy in copies[:6]:
        copy.wait()
    owner = owner_ref[...]
    carry = jnp.zeros((devices, group), F32)
    matches, ranks = [], []
    for at in range(0, count, group):
        match = (row_of == owner[:, at : at + group]).astype(F32)
        totals = dot_nn(match.astype(BF16), sums)
        ranks.append(jnp.sum(match * (totals[:, :group] + carry), axis=0, keepdims=True))
        matches.append(match)
        carry = carry + totals[:, group:]
    rank = jnp.concatenate(ranks, axis=1).astype(I32)
    match = jnp.concatenate(matches, axis=1)
    rank_ref[...] = rank

    total = jnp.zeros((1, count), F32)
    for c in range(adj_ref.shape[0]):
        mixed = dot_nn(coup_ref[...], adj_ref[c])
        total = total + jnp.sum(vel_ref[c].astype(F32) * mixed, axis=0, keepdims=True)
    product = jac_ref[...] * total

    block = block_ref[...]
    pieces = [(block >> 6).astype(F32), (block & 63).astype(F32)]
    pieces += [p.astype(F32) for p in parts(product, 3)]
    at_rank = (lax.broadcasted_iota(I32, (capacity, count), 0) == rank).astype(F32).astype(BF16)
    left = jnp.concatenate([(match * p).astype(BF16) for p in pieces], axis=0)
    placed = dot_nt(left, at_rank)
    high, low, first, second, third = [
        placed[i * devices : (i + 1) * devices] for i in range(5)
    ]
    meta = [high * 64.0 + low, first + (second + third)]
    if 2 * capacity < depth:
        meta.append(jnp.zeros((devices, depth - 2 * capacity), F32))
    meta = jnp.concatenate(meta, axis=1)

    sets = count // group
    lows = group // sets
    highs = depth // lows
    for copy in copies[6:]:
        copy.wait()
    for b in range(sets):
        off = off_ref[:, b * group : (b + 1) * group].T
        mar = mar_ref[:, b * group : (b + 1) * group].T
        first = mar.astype(BF16).astype(F32)
        high_ref[b] = off // lows
        low_ref[b] = off % lows
        first_ref[b] = first
        second_ref[b] = mar - first

    high_of = lax.broadcasted_iota(I32, (highs, entries), 0)
    low_of = lax.broadcasted_iota(I32, (lows, entries), 0)
    set_of = lax.broadcasted_iota(I32, (highs, group), 1) // lows
    unroll = 32

    def step(i, _):
        for j in range(unroll):
            g = i * unroll + j
            left, right = [], []
            for b in range(sets):
                here = jnp.broadcast_to(high_ref[b, pl.ds(g, 1), :], (highs, entries)) == high_of
                for part_ref in (first_ref, second_ref):
                    part = jnp.broadcast_to(part_ref[b, pl.ds(g, 1), :], (highs, entries))
                    left.append(jnp.where(here, part, 0.0))
                right.append(
                    (jnp.broadcast_to(low_ref[b, pl.ds(g, 1), :], (lows, entries)) == low_of).astype(F32)
                )
            both = dot_nt(
                jnp.concatenate(left, axis=0).astype(BF16),
                jnp.concatenate(right, axis=0).astype(BF16),
            )
            hist = jnp.zeros((highs, group), F32)
            for b in range(sets):
                at = 2 * highs * b
                total = both[at : at + highs] + both[at + highs : at + 2 * highs]
                hist = jnp.where(set_of == b, total, hist)
            hist_ref[pl.ds(pl.multiple_of(g * highs, highs), highs), :] = hist
        return 0

    lax.fori_loop(0, group // unroll, step, 0)
    for h in range(highs):
        turned = hist_ref[pl.ds(h, group, stride=highs), :].T
        first = turned.astype(BF16)
        second = (turned - first.astype(F32)).astype(BF16)
        for b in range(sets):
            columns = slice(b * group, (b + 1) * group)
            map_ref[h * lows : (h + 1) * lows, columns] = first[b * lows : (b + 1) * lows]
            map_ref[depth + h * lows : depth + (h + 1) * lows, columns] = second[b * lows : (b + 1) * lows]

    place = owner * stride + rank
    tile = slots // 4
    stores = []
    for at in range(0, slots, tile):
        row_of = lax.broadcasted_iota(I32, (tile, count), 0) + at
        here = (row_of == place).astype(F32).astype(BF16)
        moved = dot_nt(here, map_ref[...])
        out_ref[at : at + tile, :] = moved[:, :depth] + moved[:, depth:]
        for d in range(devices):
            row = d * stride + capacity
            if at <= row < at + tile:
                out_ref[row : row + 1, :] = meta[d : d + 1, :]
        store = pltpu.make_async_copy(
            out_ref.at[pl.ds(at, tile)], out_at.at[pl.ds(at, tile)], sems.at[at // tile]
        )
        store.start()
        stores.append(store)
    for store in stores:
        store.wait()


def constants():
    base = jnp.tanh(jnp.full((1, 1), sharpness * threshold, F32))
    return base, base + jnp.tanh(jnp.full((1, 1), sharpness * (1.0 - threshold), F32))


def slope_of(field, inverse):
    tangent = jnp.tanh(sharpness * (field - threshold))
    return sharpness * inverse * (1.0 - tangent * tangent)


def owner_kernel(odd_ref, got_ref, field_ref, val_at, y_ref, x_ref, yeven_ref, yodd_ref, dens_ref, val_ref, meta_ref, block_ref, found_ref, number_ref, sems, *, capacity, width_y):
    devices = dens_ref.shape[0]
    stride = got_ref.shape[0] // devices
    depth = got_ref.shape[1]
    rows = devices * capacity
    width_x = field_ref.shape[0] // width_y
    group = 128

    for d in range(devices):
        row = d * stride + capacity
        meta_ref[d : d + 1, :] = got_ref[row : row + 1, :]
    meta = meta_ref[...]
    block_ref[...] = meta.astype(I32)
    copy = pltpu.make_async_copy(block_ref, number_ref, sems.at[0])
    copy.start()
    prods = meta.T
    joined = group // capacity
    index = [
        jnp.concatenate(
            [block_ref[d + j : d + j + 1, :capacity] for j in range(joined)], axis=1
        )
        for d in range(0, devices, joined)
    ]
    y_of = lax.broadcasted_iota(I32, (width_y, group), 0)
    for k, part in enumerate(index):
        y_ref[:, k * group : (k + 1) * group] = (y_of == part % width_y).astype(F32).astype(BF16)
    joint = jnp.concatenate(index, axis=1)
    x_row = joint // width_y
    y_row = joint % width_y
    x_ref[...] = x_row
    copy.wait()

    def look(d, _):
        for r in range(capacity):
            found_ref[pl.ds(d * capacity + r, 1), :] = field_ref[pl.ds(number_ref[d, r], 1), :]
        return 0

    lax.fori_loop(0, devices, look, 0)

    base, ceiling = constants()
    inverse = 1.0 / ceiling
    for d in range(devices):
        at = slice(d * capacity, (d + 1) * capacity)
        tangent = jnp.tanh(sharpness * (found_ref[at, :] - threshold))
        weight = got_ref[d * stride : d * stride + capacity, :]
        high, low = parts(weight * ((base + tangent) * inverse), 2)
        val_ref[at, :depth] = high
        val_ref[at, depth:] = low
    found_ref[...] = dot_nn(val_ref[...], jnp.ones((2 * depth, depth), BF16))
    diagonal = lax.broadcasted_iota(I32, (capacity, depth), 0) == lax.broadcasted_iota(I32, (capacity, depth), 1)
    for d in range(devices):
        at = slice(d * capacity, (d + 1) * capacity)
        density = found_ref[at, :]
        dens_ref[d, :, :] = jnp.sum(jnp.where(diagonal, density, 0.0), axis=0, keepdims=True)[:, :capacity]
        shifted = ramp_q + density
        term = -ramp_q * (1.0 + ramp_q) / (shifted * shifted) * prods[capacity : 2 * capacity, d : d + 1]
        high, low = parts(term * got_ref[d * stride : d * stride + capacity, :], 2)
        val_ref[at, :depth] = high
        val_ref[at, depth:] = low

    store = pltpu.make_async_copy(val_ref, val_at, sems.at[1])
    store.start()

    x_hot = (lax.broadcasted_iota(I32, (width_x, rows), 0) == x_row).astype(F32).astype(BF16)
    ys = (0, 1, width_y - 2, width_y - 1)
    here = [
        x_hot * jnp.broadcast_to((y_row == y).astype(F32), (width_x, rows)).astype(BF16) for y in ys
    ]
    summed = dot_nn(jnp.concatenate(here, axis=0), val_ref[...])
    summed = summed[:, :depth] + summed[:, depth:]
    faces = []
    for i, y in enumerate(ys):
        field = field_ref[pl.ds(y, width_x, stride=width_y), :]
        faces.append(summed[i * width_x : (i + 1) * width_x] * slope_of(field, inverse))
    odd = odd_ref[1] == 1
    for i in range(2):
        yeven_ref[i] = jnp.where(odd, faces[i], faces[2 + i])
        yodd_ref[i] = jnp.where(odd, faces[2 + i], faces[i])
    store.wait()


def along_z(x):
    lane = lax.broadcasted_iota(I32, x.shape, x.ndim - 1)
    depth = x.shape[-1]
    up = jnp.where(lane == 0, 0.0, pltpu.roll(x, 1, x.ndim - 1))
    down = jnp.where(lane == depth - 1, 0.0, pltpu.roll(x, depth - 1, x.ndim - 1))
    return up + down


def along_rows(x, low=0.0, high=0.0):
    row = lax.broadcasted_iota(I32, x.shape, 0)
    count = x.shape[0]
    up = jnp.where(row == 0, jnp.broadcast_to(low, x.shape), pltpu.roll(x, 1, 0))
    down = jnp.where(row == count - 1, jnp.broadcast_to(high, x.shape), pltpu.roll(x, count - 1, 0))
    return up + down


def weights_of():
    center = 1.0 + 6.0 * radius_sq
    spread = relax * radius_sq / center
    scale = relax / center
    own = 1.0 - relax
    return own * (own + scale) + scale, own * spread + spread * (own + scale), spread * spread


PAD = 8


def neighbours(ref, at, inner):
    before, after = inner.start, inner.stop
    return (
        along_z(ref[at, inner, :])
        + (ref[at, before - 1 : after - 1, :] + ref[at, before + 1 : after + 1, :])
        + (ref[at - 1, inner, :] + ref[at + 1, inner, :])
    )


def step_planes(width_x):
    planes = 8
    while width_x % planes:
        planes //= 2
    return planes


def scatter_kernel(inside_ref, val_at, y_ref, x_ref, field_at, out_at, face_ref, xs_ref, ys_ref, val_ref, field_ref, wide_ref, near_ref, out_ref, sems):
    loads = fetch([val_at, field_at], [val_ref, field_ref], sems)
    rows = val_ref.shape[0]
    width_x, width_y = ys_ref.shape[0], xs_ref.shape[1]
    depth = out_ref.shape[2]
    inner = slice(PAD, PAD + width_y)
    _, ceiling = constants()
    inverse = 1.0 / ceiling
    once, near, far = weights_of()
    planes = step_planes(width_x)
    tile = planes * width_y
    steps = width_x // planes
    lead = 2 * planes + 3
    for ref in (wide_ref, near_ref):
        edges = (*range(lead), lead + width_x)
        for x in edges:
            ref[x] = jnp.zeros(ref.shape[1:], F32)
        ref[lead : lead + width_x, 0:PAD, :] = jnp.zeros((width_x, PAD, depth), F32)
        ref[lead : lead + width_x, PAD + width_y :, :] = jnp.zeros((width_x, PAD, depth), F32)
    def sums(x):
        near_ref[x, inner, :] = neighbours(wide_ref, x, inner)

    def sweeps(x):
        out_ref[x] = (
            once * wide_ref[x, inner, :]
            + near * near_ref[x, inner, :]
            + far * neighbours(near_ref, x, inner)
        )

    def store(i):
        at = i * planes
        return pltpu.make_async_copy(
            out_ref.at[pl.ds(lead + at, planes)], out_at.at[pl.ds(at, planes)], sems.at[i]
        )

    def gather(i):
        at = i * planes
        here = []
        for j in range(planes):
            at_x = (x_ref[...] == at + j).astype(F32)
            here.append(y_ref[...] * jnp.broadcast_to(at_x, (width_y, rows)).astype(BF16))
        summed = dot_nn(jnp.concatenate(here, axis=0), val_ref[...])
        return summed[:, :depth] + summed[:, depth:]

    def spread(i, summed):
        field = field_ref[pl.ds(pl.multiple_of(i * tile, tile), tile), :]
        source = summed * slope_of(field, inverse)
        wide_ref[pl.ds(lead + i * planes, planes), inner, :] = source.reshape(planes, width_y, depth)

    def step(i, _):
        at = i * planes
        for j in range(planes):
            sweeps(lead + at - 2 * planes - 2 + j)
        for j in range(planes):
            sums(lead + at - planes - 1 + j)
        near_ref[lead - 1, inner, :] = jnp.zeros((width_y, depth), F32)
        spread(i, gather(i))

        def done():
            store(i - 3).start()

        pl.when(i >= 3)(done)
        return 0

    loads[0].wait()
    summed = gather(0)
    loads[1].wait()
    spread(0, summed)
    lax.fori_loop(1, steps, step, 0)
    for x in range((steps - 1) * planes - 1, width_x):
        sums(lead + x)
    for x in range((steps - 2) * planes - 2, width_x):
        sweeps(lead + x)
    for i in range(max(0, steps - 3), steps):
        store(i).start()
    for k, x in enumerate((0, 1, width_x - 2, width_x - 1)):
        face_ref[k] = wide_ref[lead + x, inner, :]
        xs_ref[k] = out_ref[lead + x]
    xs_ref[0] = xs_ref[0] + (far * inside_ref[0]) * face_ref[0]
    xs_ref[3] = xs_ref[3] + (far * inside_ref[1]) * face_ref[3]
    block = slice(lead, lead + width_x)
    ys_ref[:, 0:PAD, :] = out_ref[block, 0:PAD, :]
    ys_ref[:, PAD : 2 * PAD, :] = out_ref[block, width_y - PAD :, :]
    for y, at, side in ((0, 0, 2), (width_y - 1, 2 * PAD - 1, 3)):
        add = (far * inside_ref[side]) * wide_ref[block, PAD + y, :]
        ys_ref[:, at, :] = ys_ref[:, at, :] + add
        for k, x in enumerate((0, 1, width_x - 2, width_x - 1)):
            row = slice(y, y + 1)
            xs_ref[k, row, :] = xs_ref[k, row, :] + add[x : x + 1]
    for i in range(steps):
        store(i).wait()


def border_kernel(inside_ref, odd_ref, partial_at, xs_ref, ys_ref, xeven_ref, xodd_ref, yeven_ref, yodd_ref, out_at, xwork_ref, ywork_ref, sems):
    width_x, _, depth = ys_ref.shape
    width_y = xs_ref.shape[1]
    _, near, far = weights_of()

    def pick(odd, even, other):
        return jnp.where(odd, even, other), jnp.where(odd, other, even)

    xodd, yodd = odd_ref[0] == 1, odd_ref[1] == 1
    xlow, xhigh = pick(xodd, xeven_ref[...], xodd_ref[...])
    ylow, yhigh = pick(yodd, yeven_ref[...], yodd_ref[...])
    low_corners = xlow[2 * width_y : 2 * width_y + 2]
    high_corners = xhigh[2 * width_y : 2 * width_y + 2]

    def layer(halo, beyond, inside, low, high):
        ring = inside * (along_z(halo) + along_rows(halo, low, high) + beyond)
        return near * halo + far * (along_z(halo) + along_rows(halo) + ring), far * halo

    def two(layers, width):
        return layers[:width], layers[width : 2 * width]

    beyond, halo = two(xlow, width_y)
    xlow = layer(halo, beyond, inside_ref[0], low_corners[0:1], low_corners[1:2])
    halo, beyond = two(xhigh, width_y)
    xhigh = layer(halo, beyond, inside_ref[1], high_corners[0:1], high_corners[1:2])
    ylow = layer(ylow[1], ylow[0], inside_ref[2], low_corners[0:1], high_corners[0:1])
    yhigh = layer(yhigh[0], yhigh[1], inside_ref[3], low_corners[1:2], high_corners[1:2])
    ywork_ref[...] = ys_ref[...]
    for y, add in ((0, ylow[0]), (1, ylow[1]), (2 * PAD - 2, yhigh[1]), (2 * PAD - 1, yhigh[0])):
        ywork_ref[:, y, :] = ywork_ref[:, y, :] + add
    for k, (x, add) in enumerate(((0, xlow[0]), (1, xlow[1]), (width_x - 2, xhigh[1]), (width_x - 1, xhigh[0]))):
        xwork_ref[k] = xs_ref[k] + add
        for y, more in ((0, ylow[0]), (1, ylow[1]), (width_y - 2, yhigh[1]), (width_y - 1, yhigh[0])):
            row = slice(y, y + 1)
            xwork_ref[k, row, :] = xwork_ref[k, row, :] + more[x : x + 1]
    middle = pl.ds(2, width_x - 4)
    stores = [
        (xwork_ref.at[pl.ds(0, 2)], out_at.at[pl.ds(0, 2)]),
        (xwork_ref.at[pl.ds(2, 2)], out_at.at[pl.ds(width_x - 2, 2)]),
        (ywork_ref.at[middle, pl.ds(0, PAD)], out_at.at[middle, pl.ds(0, PAD)]),
        (ywork_ref.at[middle, pl.ds(PAD, PAD)], out_at.at[middle, pl.ds(width_y - PAD, PAD)]),
    ]
    for store in fetch([a for a, _ in stores], [b for _, b in stores], sems):
        store.wait()


def reply_kernel(rank_ref, owner_ref, reply_ref, out_ref):
    devices, capacity = reply_ref.shape
    count = rank_ref.shape[1]
    at_rank = (lax.broadcasted_iota(I32, (capacity, count), 0) == rank_ref[...]).astype(F32).astype(BF16)
    total = jnp.zeros((devices, count), F32)
    for piece in parts(reply_ref[...], 3):
        total = total + dot_nn(piece, at_rank)
    match = lax.broadcasted_iota(I32, (devices, count), 0) == owner_ref[...]
    out_ref[...] = jnp.sum(jnp.where(match, total, 0.0), axis=0, keepdims=True)


def swap(x, axis, odd):
    count = lax.axis_size(axis)
    pairs = [(i, i + 1) for i in range(odd, count - 1, 2)]
    return lax.ppermute(x, axis, pairs + [(j, i) for i, j in pairs])


def body(velocity, adjoint, coupling, jac_weight, owner, local_block, offsets, margin, filtered):
    both = ("brick", "dom")
    brick_count = lax.axis_size("brick")
    dom_count = lax.axis_size("dom")
    devices = brick_count * dom_count
    count = owner.shape[0]
    width_x, width_y, depth = filtered.shape
    capacity = max(2, 2 * count // devices)
    slots = devices * capacity
    shape = jax.ShapeDtypeStruct
    vmem = pl.BlockSpec(memory_space=pltpu.VMEM)
    smem = pl.BlockSpec(memory_space=pltpu.SMEM)
    hbm = pl.BlockSpec(memory_space=pltpu.HBM)

    brick, dom = lax.axis_index("brick"), lax.axis_index("dom")
    inside = jnp.stack([brick > 0, brick < brick_count - 1, dom > 0, dom < dom_count - 1]).astype(F32)
    odd = jnp.stack([brick % 2, dom % 2]).astype(I32)
    owner_row = owner.reshape(1, count)
    stride = capacity + -(-2 * capacity // depth)
    lanes = 128
    turned = (count // lanes, lanes, offsets.shape[0])
    outgoing, rank = pl.pallas_call(
        functools.partial(send_kernel, devices=devices, capacity=capacity),
        out_shape=(shape((devices * stride, depth), F32), shape((1, count), I32)),
        in_specs=[hbm] * 8,
        out_specs=(hbm, vmem),
        scratch_shapes=[
            pltpu.VMEM((1, count), I32),
            pltpu.VMEM((1, count), I32),
            pltpu.VMEM((1, count), F32),
            pltpu.VMEM(velocity.shape, BF16),
            pltpu.VMEM(adjoint.shape, BF16),
            pltpu.VMEM(coupling.shape, BF16),
            pltpu.VMEM(offsets.shape, I32),
            pltpu.VMEM(margin.shape, F32),
            pltpu.VMEM(turned, I32),
            pltpu.VMEM(turned, I32),
            pltpu.VMEM(turned, F32),
            pltpu.VMEM(turned, F32),
            pltpu.VMEM((count * depth // lanes, lanes), F32),
            pltpu.VMEM((2 * depth, count), BF16),
            pltpu.VMEM((devices * stride, depth), F32),
            pltpu.SemaphoreType.DMA((8,)),
        ],
        compiler_params=params(VMEM_WHOLE),
        name="send",
    )(
        owner_row,
        local_block.reshape(1, count),
        jac_weight.reshape(1, count),
        velocity,
        adjoint,
        coupling,
        offsets,
        margin,
    )
    got = lax.all_to_all(
        outgoing.reshape(devices, 1, stride * depth), both, split_axis=0, concat_axis=0, tiled=True
    ).reshape(devices * stride, depth)
    field = filtered.reshape(width_x * width_y, depth)
    face_y = shape((2, width_x, depth), F32)
    values, y_hot, x_of, yeven, yodd, density = pl.pallas_call(
        functools.partial(owner_kernel, capacity=capacity, width_y=width_y),
        out_shape=(
            pltpu.HBM((slots, 2 * depth), BF16),
            shape((width_y, slots), BF16),
            shape((1, slots), I32),
            face_y,
            face_y,
            shape((devices, 1, capacity), F32),
        ),
        in_specs=[smem, vmem, vmem],
        out_specs=(hbm,) + (vmem,) * 5,
        scratch_shapes=[
            pltpu.VMEM((slots, 2 * depth), BF16),
            pltpu.VMEM((devices, depth), F32),
            pltpu.VMEM((devices, depth), I32),
            pltpu.VMEM((slots, depth), F32),
            pltpu.SMEM((devices, depth), I32),
            pltpu.SemaphoreType.DMA((2,)),
        ],
        compiler_params=params(),
        name="owners",
    )(odd, got, field)
    planes_x = width_x + 2 * step_planes(width_x) + 4
    wide = pltpu.VMEM((planes_x, width_y + 2 * PAD, depth), F32)
    partial, face, xs, ys = pl.pallas_call(
        scatter_kernel,
        out_shape=(
            shape(filtered.shape, F32),
            shape((4, width_y, depth), F32),
            shape((4, width_y, depth), F32),
            shape((width_x, 2 * PAD, depth), F32),
        ),
        in_specs=[smem, hbm, vmem, vmem, hbm],
        out_specs=(hbm, vmem, vmem, vmem),
        scratch_shapes=[
            pltpu.VMEM(values.shape, BF16),
            pltpu.VMEM(field.shape, F32),
            wide,
            wide,
            pltpu.VMEM((planes_x, width_y, depth), F32),
            pltpu.SemaphoreType.DMA((width_x,)),
        ],
        compiler_params=params(),
        cost_estimate=pl.CostEstimate(
            flops=8 * slots * field.size, bytes_accessed=16 * field.size, transcendentals=field.size
        ),
        name="scatter",
    )(
        inside,
        pltpu.with_memory_space_constraint(values, pltpu.HBM),
        y_hot,
        x_of,
        pltpu.with_memory_space_constraint(field, pltpu.HBM),
    )

    reply = lax.all_to_all(
        density, both, split_axis=0, concat_axis=0, tiled=True
    )
    yeven, yodd = swap(yeven, "dom", 0), swap(yodd, "dom", 1)
    dom_odd, brick_odd = dom % 2 == 1, brick % 2 == 1
    ylow, yhigh = jnp.where(dom_odd, yeven, yodd), jnp.where(dom_odd, yodd, yeven)
    filler = jnp.zeros((6, depth), F32)
    top = jnp.concatenate([face[2], face[3], ylow[1, width_x - 1 :], yhigh[0, width_x - 1 :], filler])
    bottom = jnp.concatenate([face[0], face[1], ylow[1, :1], yhigh[0, :1], filler])
    top, bottom, reply = lax.optimization_barrier((top, bottom, reply))
    xeven = swap(jnp.where(brick_odd, bottom, top), "brick", 0)
    xodd = swap(jnp.where(brick_odd, top, bottom), "brick", 1)
    element_density = pl.pallas_call(
        reply_kernel,
        out_shape=shape((1, count), F32),
        compiler_params=params(),
        name="reply",
    )(rank, owner_row, reply.reshape(devices, capacity))

    result = pl.pallas_call(
        border_kernel,
        out_shape=shape(filtered.shape, F32),
        in_specs=[smem, smem, hbm] + [vmem] * 6,
        out_specs=hbm,
        scratch_shapes=[pltpu.VMEM(xs.shape, F32), pltpu.VMEM(ys.shape, F32), pltpu.SemaphoreType.DMA((4,))],
        input_output_aliases={2: 0},
        compiler_params=params(),
        name="border",
    )(inside, odd, partial, xs, ys, xeven, xodd, yeven, yodd)
    return (result, element_density.reshape(count))


def solution(mesh):
    return jax.shard_map(
        body,
        mesh=mesh,
        in_specs=(
            P(None, None, ("brick", "dom")),
            P(None, None, ("brick", "dom")),
            P(),
            P(("brick", "dom")),
            P(("brick", "dom"), None),
            P(("brick", "dom")),
            P(None, ("brick", "dom")),
            P(None, ("brick", "dom")),
            P("brick", "dom", None),
        ),
        out_specs=(P("brick", "dom", None), P(("brick", "dom"))),
        check_vma=False,
    )
```

```python
import functools

import jax
import jax.numpy as jnp
from jax import lax
from jax.experimental import pallas as pl
from jax.experimental.pallas import tpu as pltpu
from jax.sharding import PartitionSpec as P

sharpness = 8.0
threshold = 0.5
ramp_q = 0.1
radius_sq = 1.5
relax = 0.9

VMEM_LIMIT = 32 * 1024 * 1024
VMEM_WHOLE = 60 * 1024 * 1024
BF16 = jnp.bfloat16
F32 = jnp.float32
I32 = jnp.int32


def params(limit=VMEM_LIMIT):
    return pltpu.CompilerParams(vmem_limit_bytes=limit)


def parts(x, count):
    found = []
    for _ in range(count - 1):
        head = x.astype(BF16)
        found.append(head)
        x = x - head.astype(F32)
    found.append(x.astype(BF16))
    return found


def dot_nt(a, b):
    return lax.dot_general(a, b, (((1,), (1,)), ((), ())), preferred_element_type=F32)


def dot_nn(a, b):
    return jnp.dot(a, b, preferred_element_type=F32)


def fetch(sources, targets, sems):
    copies = [
        pltpu.make_async_copy(source, target, sems.at[i])
        for i, (source, target) in enumerate(zip(sources, targets))
    ]
    for copy in copies:
        copy.start()
    return copies


def send_kernel(owner_at, block_at, jac_at, vel_at, adj_at, coup_at, off_at, mar_at, out_at, rank_ref, owner_ref, block_ref, jac_ref, vel_ref, adj_ref, coup_ref, off_ref, mar_ref, high_ref, low_ref, first_ref, second_ref, hist_ref, map_ref, out_ref, sems, *, devices, capacity):
    copies = fetch(
        [owner_at, block_at, jac_at, vel_at, adj_at, coup_at, off_at, mar_at],
        [owner_ref, block_ref, jac_ref, vel_ref, adj_ref, coup_ref, off_ref, mar_ref],
        sems,
    )
    slots, depth = out_ref.shape
    stride = slots // devices
    entries, count = off_ref.shape
    group = 128

    row_of = lax.broadcasted_iota(I32, (devices, group), 0)
    before = lax.broadcasted_iota(I32, (group, 2 * group), 0)
    after = lax.broadcasted_iota(I32, (group, 2 * group), 1)
    sums = ((before < after) | (after >= group)).astype(F32).astype(BF16)
    for copy in copies[:6]:
        copy.wait()
    owner = owner_ref[...]
    carry = jnp.zeros((devices, group), F32)
    matches, ranks = [], []
    for at in range(0, count, group):
        match = (row_of == owner[:, at : at + group]).astype(F32)
        totals = dot_nn(match.astype(BF16), sums)
        ranks.append(jnp.sum(match * (totals[:, :group] + carry), axis=0, keepdims=True))
        matches.append(match)
        carry = carry + totals[:, group:]
    rank = jnp.concatenate(ranks, axis=1).astype(I32)
    match = jnp.concatenate(matches, axis=1)
    rank_ref[...] = rank

    total = jnp.zeros((1, count), F32)
    for c in range(adj_ref.shape[0]):
        mixed = dot_nn(coup_ref[...], adj_ref[c])
        total = total + jnp.sum(vel_ref[c].astype(F32) * mixed, axis=0, keepdims=True)
    product = jac_ref[...] * total

    block = block_ref[...]
    pieces = [(block >> 6).astype(F32), (block & 63).astype(F32)]
    pieces += [p.astype(F32) for p in parts(product, 3)]
    at_rank = (lax.broadcasted_iota(I32, (capacity, count), 0) == rank).astype(F32).astype(BF16)
    left = jnp.concatenate([(match * p).astype(BF16) for p in pieces], axis=0)
    placed = dot_nt(left, at_rank)
    high, low, first, second, third = [
        placed[i * devices : (i + 1) * devices] for i in range(5)
    ]
    meta = [high * 64.0 + low, first + (second + third)]
    if 2 * capacity < depth:
        meta.append(jnp.zeros((devices, depth - 2 * capacity), F32))
    meta = jnp.concatenate(meta, axis=1)

    sets = count // group
    lows = group // sets
    highs = depth // lows
    for copy in copies[6:]:
        copy.wait()
    for b in range(sets):
        off = off_ref[:, b * group : (b + 1) * group].T
        mar = mar_ref[:, b * group : (b + 1) * group].T
        first = mar.astype(BF16).astype(F32)
        high_ref[b] = off // lows
        low_ref[b] = off % lows
        first_ref[b] = first
        second_ref[b] = mar - first

    high_of = lax.broadcasted_iota(I32, (highs, entries), 0)
    low_of = lax.broadcasted_iota(I32, (lows, entries), 0)
    set_of = lax.broadcasted_iota(I32, (highs, group), 1) // lows
    unroll = 64

    def step(i, _):
        for j in range(unroll):
            g = i * unroll + j
            left, right = [], []
            for b in range(sets):
                here = jnp.broadcast_to(high_ref[b, pl.ds(g, 1), :], (highs, entries)) == high_of
                for part_ref in (first_ref, second_ref):
                    part = jnp.broadcast_to(part_ref[b, pl.ds(g, 1), :], (highs, entries))
                    left.append(jnp.where(here, part, 0.0))
                right.append(
                    (jnp.broadcast_to(low_ref[b, pl.ds(g, 1), :], (lows, entries)) == low_of).astype(F32)
                )
            both = dot_nn(
                jnp.concatenate(left, axis=0).astype(BF16),
                jnp.concatenate(right, axis=0).T.astype(BF16),
            )
            hist = jnp.zeros((highs, group), F32)
            for b in range(sets):
                at = 2 * highs * b
                total = both[at : at + highs] + both[at + highs : at + 2 * highs]
                hist = jnp.where(set_of == b, total, hist)
            hist_ref[pl.ds(pl.multiple_of(g * highs, highs), highs), :] = hist
        return 0

    lax.fori_loop(0, group // unroll, step, 0)
    for h in range(highs):
        turned = hist_ref[pl.ds(h, group, stride=highs), :].T
        first = turned.astype(BF16)
        second = (turned - first.astype(F32)).astype(BF16)
        for b in range(sets):
            columns = slice(b * group, (b + 1) * group)
            map_ref[h * lows : (h + 1) * lows, columns] = first[b * lows : (b + 1) * lows]
            map_ref[depth + h * lows : depth + (h + 1) * lows, columns] = second[b * lows : (b + 1) * lows]

    place = owner * stride + rank
    tile = slots // 4
    stores = []
    for at in range(0, slots, tile):
        row_of = lax.broadcasted_iota(I32, (tile, count), 0) + at
        here = (row_of == place).astype(F32).astype(BF16)
        moved = dot_nt(here, map_ref[...])
        out_ref[at : at + tile, :] = moved[:, :depth] + moved[:, depth:]
        for d in range(devices):
            row = d * stride + capacity
            if at <= row < at + tile:
                out_ref[row : row + 1, :] = meta[d : d + 1, :]
        store = pltpu.make_async_copy(
            out_ref.at[pl.ds(at, tile)], out_at.at[pl.ds(at, tile)], sems.at[at // tile]
        )
        store.start()
        stores.append(store)
    for store in stores:
        store.wait()


def constants():
    base = jnp.tanh(jnp.full((1, 1), sharpness * threshold, F32))
    return base, base + jnp.tanh(jnp.full((1, 1), sharpness * (1.0 - threshold), F32))


def slope_of(field, inverse):
    tangent = jnp.tanh(sharpness * (field - threshold))
    return sharpness * inverse * (1.0 - tangent * tangent)


def owner_kernel(odd_ref, got_ref, field_at, val_ref, y_ref, x_ref, yeven_ref, yodd_ref, dens_ref, meta_ref, block_ref, found_ref, number_ref, field_ref, layers_ref, sem, load_sem, *, capacity, width_y):
    load = pltpu.make_async_copy(field_at, field_ref, load_sem)
    load.start()
    devices = dens_ref.shape[0]
    stride = got_ref.shape[0] // devices
    depth = got_ref.shape[1]
    rows = devices * capacity
    width_x = field_ref.shape[0] // width_y
    group = 128

    for d in range(devices):
        row = d * stride + capacity
        meta_ref[d : d + 1, :] = got_ref[row : row + 1, :]
    meta = meta_ref[...]
    block_ref[...] = meta.astype(I32)
    copy = pltpu.make_async_copy(block_ref, number_ref, sem)
    copy.start()
    prods = meta.T
    joined = group // capacity
    index = [
        jnp.concatenate(
            [block_ref[d + j : d + j + 1, :capacity] for j in range(joined)], axis=1
        )
        for d in range(0, devices, joined)
    ]
    y_of = lax.broadcasted_iota(I32, (width_y, group), 0)
    for k, part in enumerate(index):
        y_ref[:, k * group : (k + 1) * group] = (y_of == part % width_y).astype(F32).astype(BF16)
    joint = jnp.concatenate(index, axis=1)
    x_row = joint // width_y
    y_row = joint % width_y
    x_ref[...] = x_row
    x_hot = (lax.broadcasted_iota(I32, (width_x, rows), 0) == x_row).astype(F32).astype(BF16)
    ys = (0, 1, width_y - 2, width_y - 1)
    for i, y in enumerate(ys):
        at_y = jnp.broadcast_to((y_row == y).astype(F32), (width_x, rows)).astype(BF16)
        layers_ref[i * width_x : (i + 1) * width_x, :] = x_hot * at_y
    copy.wait()
    load.wait()

    def look(d, _):
        for r in range(capacity):
            found_ref[pl.ds(d * capacity + r, 1), :] = field_ref[pl.ds(number_ref[d, r], 1), :]
        return 0

    lax.fori_loop(0, devices, look, 0)

    base, ceiling = constants()
    inverse = 1.0 / ceiling
    for d in range(devices):
        at = slice(d * capacity, (d + 1) * capacity)
        tangent = jnp.tanh(sharpness * (found_ref[at, :] - threshold))
        weight = got_ref[d * stride : d * stride + capacity, :]
        high, low = parts(weight * ((base + tangent) * inverse), 2)
        val_ref[at, :depth] = high
        val_ref[at, depth:] = low
    found_ref[...] = dot_nn(val_ref[...], jnp.ones((2 * depth, depth), BF16))
    diagonal = lax.broadcasted_iota(I32, (capacity, depth), 0) == lax.broadcasted_iota(I32, (capacity, depth), 1)
    for d in range(devices):
        at = slice(d * capacity, (d + 1) * capacity)
        density = found_ref[at, :]
        dens_ref[d, :, :] = jnp.sum(jnp.where(diagonal, density, 0.0), axis=0, keepdims=True)[:, :capacity]
        shifted = ramp_q + density
        term = -ramp_q * (1.0 + ramp_q) / (shifted * shifted) * prods[capacity : 2 * capacity, d : d + 1]
        high, low = parts(term * got_ref[d * stride : d * stride + capacity, :], 2)
        val_ref[at, :depth] = high
        val_ref[at, depth:] = low

    summed = dot_nn(layers_ref[...], val_ref[...])
    summed = summed[:, :depth] + summed[:, depth:]
    faces = []
    for i, y in enumerate(ys):
        field = field_ref[pl.ds(y, width_x, stride=width_y), :]
        faces.append(summed[i * width_x : (i + 1) * width_x] * slope_of(field, inverse))
    odd = odd_ref[1] == 1
    for i in range(2):
        yeven_ref[i] = jnp.where(odd, faces[i], faces[2 + i])
        yodd_ref[i] = jnp.where(odd, faces[2 + i], faces[i])


def along_z(x):
    lane = lax.broadcasted_iota(I32, x.shape, x.ndim - 1)
    depth = x.shape[-1]
    up = jnp.where(lane == 0, 0.0, pltpu.roll(x, 1, x.ndim - 1))
    down = jnp.where(lane == depth - 1, 0.0, pltpu.roll(x, depth - 1, x.ndim - 1))
    return up + down


def along_rows(x, low=0.0, high=0.0):
    row = lax.broadcasted_iota(I32, x.shape, 0)
    count = x.shape[0]
    up = jnp.where(row == 0, jnp.broadcast_to(low, x.shape), pltpu.roll(x, 1, 0))
    down = jnp.where(row == count - 1, jnp.broadcast_to(high, x.shape), pltpu.roll(x, count - 1, 0))
    return up + down


def weights_of():
    center = 1.0 + 6.0 * radius_sq
    spread = relax * radius_sq / center
    scale = relax / center
    own = 1.0 - relax
    return own * (own + scale) + scale, own * spread + spread * (own + scale), spread * spread


PAD = 8


def neighbours(ref, at, inner):
    before, after = inner.start, inner.stop
    return (
        along_z(ref[at, inner, :])
        + (ref[at, before - 1 : after - 1, :] + ref[at, before + 1 : after + 1, :])
        + (ref[at - 1, inner, :] + ref[at + 1, inner, :])
    )


def step_planes(width_x):
    planes = 8
    while width_x % planes:
        planes //= 2
    return planes


def scatter_kernel(inside_ref, val_ref, y_ref, x_ref, field_at, out_at, face_ref, xs_ref, ys_ref, field_ref, wide_ref, near_ref, out_ref, sems):
    rows = val_ref.shape[0]
    width_x, width_y = ys_ref.shape[0], xs_ref.shape[1]
    depth = out_ref.shape[2]
    inner = slice(PAD, PAD + width_y)
    _, ceiling = constants()
    inverse = 1.0 / ceiling
    once, near, far = weights_of()
    planes = step_planes(width_x)
    tile = planes * width_y
    steps = width_x // planes
    lead = 2 * planes + 3

    def load(i):
        at = pl.ds(pl.multiple_of(i * tile, tile), tile)
        return pltpu.make_async_copy(field_at.at[at], field_ref.at[at], sems.at[steps + i])

    for i in range(steps):
        load(i).start()
    for ref in (wide_ref, near_ref):
        edges = (*range(lead), lead + width_x)
        for x in edges:
            ref[x] = jnp.zeros(ref.shape[1:], F32)
        ref[lead : lead + width_x, 0:PAD, :] = jnp.zeros((width_x, PAD, depth), F32)
        ref[lead : lead + width_x, PAD + width_y :, :] = jnp.zeros((width_x, PAD, depth), F32)
    def sums(x):
        near_ref[x, inner, :] = neighbours(wide_ref, x, inner)

    def sweeps(x):
        out_ref[x] = (
            once * wide_ref[x, inner, :]
            + near * near_ref[x, inner, :]
            + far * neighbours(near_ref, x, inner)
        )

    def store(i):
        at = i * planes
        return pltpu.make_async_copy(
            out_ref.at[pl.ds(lead + at, planes)], out_at.at[pl.ds(at, planes)], sems.at[i]
        )

    def gather(i):
        at = i * planes
        here = []
        for j in range(planes):
            at_x = (x_ref[...] == at + j).astype(F32)
            here.append(y_ref[...] * jnp.broadcast_to(at_x, (width_y, rows)).astype(BF16))
        summed = dot_nn(jnp.concatenate(here, axis=0), val_ref[...])
        return summed[:, :depth] + summed[:, depth:]

    def spread(i, summed):
        field = field_ref[pl.ds(pl.multiple_of(i * tile, tile), tile), :]
        source = summed * slope_of(field, inverse)
        wide_ref[pl.ds(lead + i * planes, planes), inner, :] = source.reshape(planes, width_y, depth)

    def step(i, _):
        load(i).wait()
        at = i * planes
        for j in range(planes):
            sweeps(lead + at - 2 * planes - 2 + j)
        for j in range(planes):
            sums(lead + at - planes - 1 + j)
        near_ref[lead - 1, inner, :] = jnp.zeros((width_y, depth), F32)
        spread(i, gather(i))

        def done():
            store(i - 3).start()

        pl.when(i >= 3)(done)
        return 0

    summed = gather(0)
    load(0).wait()
    spread(0, summed)
    lax.fori_loop(1, steps, step, 0)
    for x in range((steps - 1) * planes - 1, width_x):
        sums(lead + x)
    for x in range((steps - 2) * planes - 2, width_x):
        sweeps(lead + x)
    for i in range(max(0, steps - 3), steps):
        store(i).start()
    for k, x in enumerate((0, 1, width_x - 2, width_x - 1)):
        face_ref[k] = wide_ref[lead + x, inner, :]
        xs_ref[k] = out_ref[lead + x]
    xs_ref[0] = xs_ref[0] + (far * inside_ref[0]) * face_ref[0]
    xs_ref[3] = xs_ref[3] + (far * inside_ref[1]) * face_ref[3]
    block = slice(lead, lead + width_x)
    ys_ref[:, 0:PAD, :] = out_ref[block, 0:PAD, :]
    ys_ref[:, PAD : 2 * PAD, :] = out_ref[block, width_y - PAD :, :]
    for y, at, side in ((0, 0, 2), (width_y - 1, 2 * PAD - 1, 3)):
        add = (far * inside_ref[side]) * wide_ref[block, PAD + y, :]
        ys_ref[:, at, :] = ys_ref[:, at, :] + add
        for k, x in enumerate((0, 1, width_x - 2, width_x - 1)):
            row = slice(y, y + 1)
            xs_ref[k, row, :] = xs_ref[k, row, :] + add[x : x + 1]
    for i in range(steps):
        store(i).wait()


def border_kernel(inside_ref, odd_ref, partial_at, xs_ref, ys_ref, xeven_ref, xodd_ref, yeven_ref, yodd_ref, out_at, xwork_ref, ywork_ref, sems):
    width_x, _, depth = ys_ref.shape
    width_y = xs_ref.shape[1]
    _, near, far = weights_of()

    def pick(odd, even, other):
        return jnp.where(odd, even, other), jnp.where(odd, other, even)

    xodd, yodd = odd_ref[0] == 1, odd_ref[1] == 1
    xlow, xhigh = pick(xodd, xeven_ref[...], xodd_ref[...])
    ylow, yhigh = pick(yodd, yeven_ref[...], yodd_ref[...])
    low_corners = xlow[2 * width_y : 2 * width_y + 2]
    high_corners = xhigh[2 * width_y : 2 * width_y + 2]

    def layer(halo, beyond, inside, low, high):
        ring = inside * (along_z(halo) + along_rows(halo, low, high) + beyond)
        return near * halo + far * (along_z(halo) + along_rows(halo) + ring), far * halo

    def two(layers, width):
        return layers[:width], layers[width : 2 * width]

    beyond, halo = two(xlow, width_y)
    xlow = layer(halo, beyond, inside_ref[0], low_corners[0:1], low_corners[1:2])
    halo, beyond = two(xhigh, width_y)
    xhigh = layer(halo, beyond, inside_ref[1], high_corners[0:1], high_corners[1:2])
    ylow = layer(ylow[1], ylow[0], inside_ref[2], low_corners[0:1], high_corners[0:1])
    yhigh = layer(yhigh[0], yhigh[1], inside_ref[3], low_corners[1:2], high_corners[1:2])
    ywork_ref[...] = ys_ref[...]
    for y, add in ((0, ylow[0]), (1, ylow[1]), (2 * PAD - 2, yhigh[1]), (2 * PAD - 1, yhigh[0])):
        ywork_ref[:, y, :] = ywork_ref[:, y, :] + add
    for k, (x, add) in enumerate(((0, xlow[0]), (1, xlow[1]), (width_x - 2, xhigh[1]), (width_x - 1, xhigh[0]))):
        xwork_ref[k] = xs_ref[k] + add
        for y, more in ((0, ylow[0]), (1, ylow[1]), (width_y - 2, yhigh[1]), (width_y - 1, yhigh[0])):
            row = slice(y, y + 1)
            xwork_ref[k, row, :] = xwork_ref[k, row, :] + more[x : x + 1]
    middle = pl.ds(2, width_x - 4)
    stores = [
        (xwork_ref.at[pl.ds(0, 2)], out_at.at[pl.ds(0, 2)]),
        (xwork_ref.at[pl.ds(2, 2)], out_at.at[pl.ds(width_x - 2, 2)]),
        (ywork_ref.at[middle, pl.ds(0, PAD)], out_at.at[middle, pl.ds(0, PAD)]),
        (ywork_ref.at[middle, pl.ds(PAD, PAD)], out_at.at[middle, pl.ds(width_y - PAD, PAD)]),
    ]
    for store in fetch([a for a, _ in stores], [b for _, b in stores], sems):
        store.wait()


def reply_kernel(rank_ref, owner_ref, reply_ref, out_ref):
    devices, capacity = reply_ref.shape
    count = rank_ref.shape[1]
    at_rank = (lax.broadcasted_iota(I32, (capacity, count), 0) == rank_ref[...]).astype(F32).astype(BF16)
    total = jnp.zeros((devices, count), F32)
    for piece in parts(reply_ref[...], 3):
        total = total + dot_nn(piece, at_rank)
    match = lax.broadcasted_iota(I32, (devices, count), 0) == owner_ref[...]
    out_ref[...] = jnp.sum(jnp.where(match, total, 0.0), axis=0, keepdims=True)


def swap(x, axis, odd):
    count = lax.axis_size(axis)
    pairs = [(i, i + 1) for i in range(odd, count - 1, 2)]
    return lax.ppermute(x, axis, pairs + [(j, i) for i, j in pairs])


def body(velocity, adjoint, coupling, jac_weight, owner, local_block, offsets, margin, filtered):
    both = ("brick", "dom")
    brick_count = lax.axis_size("brick")
    dom_count = lax.axis_size("dom")
    devices = brick_count * dom_count
    count = owner.shape[0]
    width_x, width_y, depth = filtered.shape
    capacity = max(2, 2 * count // devices)
    slots = devices * capacity
    shape = jax.ShapeDtypeStruct
    vmem = pl.BlockSpec(memory_space=pltpu.VMEM)
    smem = pl.BlockSpec(memory_space=pltpu.SMEM)
    hbm = pl.BlockSpec(memory_space=pltpu.HBM)

    brick, dom = lax.axis_index("brick"), lax.axis_index("dom")
    inside = jnp.stack([brick > 0, brick < brick_count - 1, dom > 0, dom < dom_count - 1]).astype(F32)
    odd = jnp.stack([brick % 2, dom % 2]).astype(I32)
    owner_row = owner.reshape(1, count)
    stride = capacity + -(-2 * capacity // depth)
    lanes = 128
    turned = (count // lanes, lanes, offsets.shape[0])
    outgoing, rank = pl.pallas_call(
        functools.partial(send_kernel, devices=devices, capacity=capacity),
        out_shape=(shape((devices * stride, depth), F32), shape((1, count), I32)),
        in_specs=[hbm] * 8,
        out_specs=(hbm, vmem),
        scratch_shapes=[
            pltpu.VMEM((1, count), I32),
            pltpu.VMEM((1, count), I32),
            pltpu.VMEM((1, count), F32),
            pltpu.VMEM(velocity.shape, BF16),
            pltpu.VMEM(adjoint.shape, BF16),
            pltpu.VMEM(coupling.shape, BF16),
            pltpu.VMEM(offsets.shape, I32),
            pltpu.VMEM(margin.shape, F32),
            pltpu.VMEM(turned, I32),
            pltpu.VMEM(turned, I32),
            pltpu.VMEM(turned, F32),
            pltpu.VMEM(turned, F32),
            pltpu.VMEM((count * depth // lanes, lanes), F32),
            pltpu.VMEM((2 * depth, count), BF16),
            pltpu.VMEM((devices * stride, depth), F32),
            pltpu.SemaphoreType.DMA((8,)),
        ],
        compiler_params=params(VMEM_WHOLE),
        name="send",
    )(
        owner_row,
        local_block.reshape(1, count),
        jac_weight.reshape(1, count),
        velocity,
        adjoint,
        coupling,
        offsets,
        margin,
    )
    got = lax.all_to_all(
        outgoing.reshape(devices, 1, stride * depth), both, split_axis=0, concat_axis=0, tiled=True
    ).reshape(devices * stride, depth)
    field = filtered.reshape(width_x * width_y, depth)
    face_y = shape((2, width_x, depth), F32)
    values, y_hot, x_of, yeven, yodd, density = pl.pallas_call(
        functools.partial(owner_kernel, capacity=capacity, width_y=width_y),
        out_shape=(
            shape((slots, 2 * depth), BF16),
            shape((width_y, slots), BF16),
            shape((1, slots), I32),
            face_y,
            face_y,
            shape((devices, 1, capacity), F32),
        ),
        in_specs=[smem, vmem, hbm],
        out_specs=(vmem,) * 6,
        scratch_shapes=[
            pltpu.VMEM((devices, depth), F32),
            pltpu.VMEM((devices, depth), I32),
            pltpu.VMEM((slots, depth), F32),
            pltpu.SMEM((devices, depth), I32),
            pltpu.VMEM(field.shape, F32),
            pltpu.VMEM((4 * width_x, slots), BF16),
            pltpu.SemaphoreType.DMA,
            pltpu.SemaphoreType.DMA,
        ],
        compiler_params=params(),
        name="owners",
    )(odd, got, pltpu.with_memory_space_constraint(field, pltpu.HBM))
    planes_x = width_x + 2 * step_planes(width_x) + 4
    wide = pltpu.VMEM((planes_x, width_y + 2 * PAD, depth), F32)
    partial, face, xs, ys = pl.pallas_call(
        scatter_kernel,
        out_shape=(
            shape(filtered.shape, F32),
            shape((4, width_y, depth), F32),
            shape((4, width_y, depth), F32),
            shape((width_x, 2 * PAD, depth), F32),
        ),
        in_specs=[smem, vmem, vmem, vmem, hbm],
        out_specs=(hbm, vmem, vmem, vmem),
        scratch_shapes=[
            pltpu.VMEM(field.shape, F32),
            wide,
            wide,
            pltpu.VMEM((planes_x, width_y, depth), F32),
            pltpu.SemaphoreType.DMA((2 * width_x // step_planes(width_x),)),
        ],
        compiler_params=params(),
        cost_estimate=pl.CostEstimate(
            flops=8 * slots * field.size, bytes_accessed=16 * field.size, transcendentals=field.size
        ),
        name="scatter",
    )(inside, values, y_hot, x_of, pltpu.with_memory_space_constraint(field, pltpu.HBM))

    reply = lax.all_to_all(
        density, both, split_axis=0, concat_axis=0, tiled=True
    )
    yeven, yodd = swap(yeven, "dom", 0), swap(yodd, "dom", 1)
    dom_odd, brick_odd = dom % 2 == 1, brick % 2 == 1
    ylow, yhigh = jnp.where(dom_odd, yeven, yodd), jnp.where(dom_odd, yodd, yeven)
    filler = jnp.zeros((6, depth), F32)
    top = jnp.concatenate([face[2], face[3], ylow[1, width_x - 1 :], yhigh[0, width_x - 1 :], filler])
    bottom = jnp.concatenate([face[0], face[1], ylow[1, :1], yhigh[0, :1], filler])
    top, bottom, reply = lax.optimization_barrier((top, bottom, reply))
    xeven = swap(jnp.where(brick_odd, bottom, top), "brick", 0)
    xodd = swap(jnp.where(brick_odd, top, bottom), "brick", 1)
    element_density = pl.pallas_call(
        reply_kernel,
        out_shape=shape((1, count), F32),
        compiler_params=params(),
        name="reply",
    )(rank, owner_row, reply.reshape(devices, capacity))

    result = pl.pallas_call(
        border_kernel,
        out_shape=shape(filtered.shape, F32),
        in_specs=[smem, smem, hbm] + [vmem] * 6,
        out_specs=hbm,
        scratch_shapes=[pltpu.VMEM(xs.shape, F32), pltpu.VMEM(ys.shape, F32), pltpu.SemaphoreType.DMA((4,))],
        input_output_aliases={2: 0},
        compiler_params=params(),
        name="border",
    )(inside, odd, partial, xs, ys, xeven, xodd, yeven, yodd)
    return (result, element_density.reshape(count))


def solution(mesh):
    return jax.shard_map(
        body,
        mesh=mesh,
        in_specs=(
            P(None, None, ("brick", "dom")),
            P(None, None, ("brick", "dom")),
            P(),
            P(("brick", "dom")),
            P(("brick", "dom"), None),
            P(("brick", "dom")),
            P(None, ("brick", "dom")),
            P(None, ("brick", "dom")),
            P("brick", "dom", None),
        ),
        out_specs=(P("brick", "dom", None), P(("brick", "dom"))),
        check_vma=False,
    )
```

```python
import functools

import jax
import jax.numpy as jnp
from jax import lax
from jax.experimental import pallas as pl
from jax.experimental.pallas import tpu as pltpu
from jax.sharding import PartitionSpec as P

sharpness = 8.0
threshold = 0.5
ramp_q = 0.1
radius_sq = 1.5
relax = 0.9

VMEM_LIMIT = 32 * 1024 * 1024
VMEM_WHOLE = 60 * 1024 * 1024
BF16 = jnp.bfloat16
F32 = jnp.float32
I32 = jnp.int32


def params(limit=VMEM_LIMIT):
    return pltpu.CompilerParams(vmem_limit_bytes=limit)


def parts(x, count):
    found = []
    for _ in range(count - 1):
        head = x.astype(BF16)
        found.append(head)
        x = x - head.astype(F32)
    found.append(x.astype(BF16))
    return found


def dot_nt(a, b):
    return lax.dot_general(a, b, (((1,), (1,)), ((), ())), preferred_element_type=F32)


def dot_nn(a, b):
    return jnp.dot(a, b, preferred_element_type=F32)


def fetch(sources, targets, sems):
    copies = [
        pltpu.make_async_copy(source, target, sems.at[i])
        for i, (source, target) in enumerate(zip(sources, targets))
    ]
    for copy in copies:
        copy.start()
    return copies


def send_kernel(owner_at, block_at, jac_at, vel_at, adj_at, coup_at, off_at, mar_at, out_ref, rank_ref, owner_ref, block_ref, jac_ref, vel_ref, adj_ref, coup_ref, off_ref, mar_ref, high_ref, low_ref, first_ref, second_ref, hist_ref, map_ref, sems, *, devices, capacity):
    copies = fetch(
        [owner_at, block_at, jac_at, vel_at, adj_at, coup_at, off_at, mar_at],
        [owner_ref, block_ref, jac_ref, vel_ref, adj_ref, coup_ref, off_ref, mar_ref],
        sems,
    )
    slots, depth = out_ref.shape
    stride = slots // devices
    entries, count = off_ref.shape
    group = 128

    row_of = lax.broadcasted_iota(I32, (devices, group), 0)
    before = lax.broadcasted_iota(I32, (group, 2 * group), 0)
    after = lax.broadcasted_iota(I32, (group, 2 * group), 1)
    sums = ((before < after) | (after >= group)).astype(F32).astype(BF16)
    for copy in copies[:6]:
        copy.wait()
    owner = owner_ref[...]
    carry = jnp.zeros((devices, group), F32)
    matches, ranks = [], []
    for at in range(0, count, group):
        match = (row_of == owner[:, at : at + group]).astype(F32)
        totals = dot_nn(match.astype(BF16), sums)
        ranks.append(jnp.sum(match * (totals[:, :group] + carry), axis=0, keepdims=True))
        matches.append(match)
        carry = carry + totals[:, group:]
    rank = jnp.concatenate(ranks, axis=1).astype(I32)
    match = jnp.concatenate(matches, axis=1)
    rank_ref[...] = rank

    total = jnp.zeros((1, count), F32)
    for c in range(adj_ref.shape[0]):
        mixed = dot_nn(coup_ref[...], adj_ref[c])
        total = total + jnp.sum(vel_ref[c].astype(F32) * mixed, axis=0, keepdims=True)
    product = jac_ref[...] * total

    block = block_ref[...]
    pieces = [(block >> 6).astype(F32), (block & 63).astype(F32)]
    pieces += [p.astype(F32) for p in parts(product, 3)]
    at_rank = (lax.broadcasted_iota(I32, (capacity, count), 0) == rank).astype(F32).astype(BF16)
    left = jnp.concatenate([(match * p).astype(BF16) for p in pieces], axis=0)
    placed = dot_nt(left, at_rank)
    high, low, first, second, third = [
        placed[i * devices : (i + 1) * devices] for i in range(5)
    ]
    meta = [high * 64.0 + low, first + (second + third)]
    if 2 * capacity < depth:
        meta.append(jnp.zeros((devices, depth - 2 * capacity), F32))
    meta = jnp.concatenate(meta, axis=1)

    sets = count // group
    lows = group // sets
    highs = depth // lows
    for copy in copies[6:]:
        copy.wait()
    for b in range(sets):
        off = off_ref[:, b * group : (b + 1) * group].T
        mar = mar_ref[:, b * group : (b + 1) * group].T
        first = mar.astype(BF16).astype(F32)
        high_ref[b] = off // lows
        low_ref[b] = off % lows
        first_ref[b] = first
        second_ref[b] = mar - first

    high_of = lax.broadcasted_iota(I32, (highs, entries), 0)
    low_of = lax.broadcasted_iota(I32, (lows, entries), 0)
    set_of = lax.broadcasted_iota(I32, (highs, group), 1) // lows
    unroll = 64

    def step(i, _):
        for j in range(unroll):
            g = i * unroll + j
            left, right = [], []
            for b in range(sets):
                here = jnp.broadcast_to(high_ref[b, pl.ds(g, 1), :], (highs, entries)) == high_of
                for part_ref in (first_ref, second_ref):
                    part = jnp.broadcast_to(part_ref[b, pl.ds(g, 1), :], (highs, entries))
                    left.append(jnp.where(here, part, 0.0))
                right.append(
                    (jnp.broadcast_to(low_ref[b, pl.ds(g, 1), :], (lows, entries)) == low_of).astype(F32)
                )
            both = dot_nn(
                jnp.concatenate(left, axis=0).astype(BF16),
                jnp.concatenate(right, axis=0).T.astype(BF16),
            )
            hist = jnp.zeros((highs, group), F32)
            for b in range(sets):
                at = 2 * highs * b
                total = both[at : at + highs] + both[at + highs : at + 2 * highs]
                hist = jnp.where(set_of == b, total, hist)
            hist_ref[pl.ds(pl.multiple_of(g * highs, highs), highs), :] = hist
        return 0

    lax.fori_loop(0, group // unroll, step, 0)
    for h in range(highs):
        turned = hist_ref[pl.ds(h, group, stride=highs), :].T
        first = turned.astype(BF16)
        second = (turned - first.astype(F32)).astype(BF16)
        for b in range(sets):
            columns = slice(b * group, (b + 1) * group)
            map_ref[h * lows : (h + 1) * lows, columns] = first[b * lows : (b + 1) * lows]
            map_ref[depth + h * lows : depth + (h + 1) * lows, columns] = second[b * lows : (b + 1) * lows]

    place = owner * stride + rank
    tile = slots // 4
    for at in range(0, slots, tile):
        row_of = lax.broadcasted_iota(I32, (tile, count), 0) + at
        here = (row_of == place).astype(F32).astype(BF16)
        moved = dot_nt(here, map_ref[...])
        out_ref[at : at + tile, :] = moved[:, :depth] + moved[:, depth:]
        for d in range(devices):
            row = d * stride + capacity
            if at <= row < at + tile:
                out_ref[row : row + 1, :] = meta[d : d + 1, :]


def constants():
    base = jnp.tanh(jnp.full((1, 1), sharpness * threshold, F32))
    return base, base + jnp.tanh(jnp.full((1, 1), sharpness * (1.0 - threshold), F32))


def slope_of(field, inverse):
    tangent = jnp.tanh(sharpness * (field - threshold))
    return sharpness * inverse * (1.0 - tangent * tangent)


def owner_kernel(odd_ref, number_ref, got_ref, field_ref, given_ref, index_ref, yeven_ref, yodd_ref, dens_ref, meta_ref, block_ref, found_ref, val_ref, layers_ref, *, capacity, width_y):
    devices = dens_ref.shape[0]
    stride = got_ref.shape[0] // devices
    depth = got_ref.shape[1]
    rows = devices * capacity
    width_x = field_ref.shape[0] // width_y
    group = 128

    for d in range(devices):
        row = d * stride + capacity
        meta_ref[d : d + 1, :] = got_ref[row : row + 1, :]
    meta = meta_ref[...]
    block_ref[...] = meta.astype(I32)
    prods = meta.T
    joined = group // capacity
    index = [
        jnp.concatenate(
            [block_ref[d + j : d + j + 1, :capacity] for j in range(joined)], axis=1
        )
        for d in range(0, devices, joined)
    ]
    joint = jnp.concatenate(index, axis=1)
    x_row = joint // width_y
    y_row = joint % width_y
    index_ref[...] = joint
    x_hot = (lax.broadcasted_iota(I32, (width_x, rows), 0) == x_row).astype(F32).astype(BF16)
    ys = (0, 1, width_y - 2, width_y - 1)
    for i, y in enumerate(ys):
        at_y = jnp.broadcast_to((y_row == y).astype(F32), (width_x, rows)).astype(BF16)
        layers_ref[i * width_x : (i + 1) * width_x, :] = x_hot * at_y

    def look(d, _):
        for r in range(capacity):
            found_ref[pl.ds(d * capacity + r, 1), :] = field_ref[pl.ds(number_ref[d, r], 1), :]
        return 0

    lax.fori_loop(0, devices, look, 0)

    base, ceiling = constants()
    inverse = 1.0 / ceiling
    for d in range(devices):
        at = slice(d * capacity, (d + 1) * capacity)
        tangent = jnp.tanh(sharpness * (found_ref[at, :] - threshold))
        weight = got_ref[d * stride : d * stride + capacity, :]
        high, low = parts(weight * ((base + tangent) * inverse), 2)
        val_ref[at, :depth] = high
        val_ref[at, depth:] = low
    found_ref[...] = dot_nn(val_ref[...], jnp.ones((2 * depth, depth), BF16))
    diagonal = lax.broadcasted_iota(I32, (capacity, depth), 0) == lax.broadcasted_iota(I32, (capacity, depth), 1)
    for d in range(devices):
        at = slice(d * capacity, (d + 1) * capacity)
        density = found_ref[at, :]
        dens_ref[d, :, :] = jnp.sum(jnp.where(diagonal, density, 0.0), axis=0, keepdims=True)[:, :capacity]
        shifted = ramp_q + density
        term = -ramp_q * (1.0 + ramp_q) / (shifted * shifted) * prods[capacity : 2 * capacity, d : d + 1]
        value = term * got_ref[d * stride : d * stride + capacity, :]
        given_ref[d * stride : d * stride + capacity, :] = value
        high, low = parts(value, 2)
        val_ref[at, :depth] = high
        val_ref[at, depth:] = low

    summed = dot_nn(layers_ref[...], val_ref[...])
    summed = summed[:, :depth] + summed[:, depth:]
    faces = []
    for i, y in enumerate(ys):
        field = field_ref[pl.ds(y, width_x, stride=width_y), :]
        faces.append(summed[i * width_x : (i + 1) * width_x] * slope_of(field, inverse))
    odd = odd_ref[1] == 1
    for i in range(2):
        yeven_ref[i] = jnp.where(odd, faces[i], faces[2 + i])
        yodd_ref[i] = jnp.where(odd, faces[2 + i], faces[i])


def along_z(x):
    lane = lax.broadcasted_iota(I32, x.shape, x.ndim - 1)
    depth = x.shape[-1]
    up = jnp.where(lane == 0, 0.0, pltpu.roll(x, 1, x.ndim - 1))
    down = jnp.where(lane == depth - 1, 0.0, pltpu.roll(x, depth - 1, x.ndim - 1))
    return up + down


def along_rows(x, low=0.0, high=0.0):
    row = lax.broadcasted_iota(I32, x.shape, 0)
    count = x.shape[0]
    up = jnp.where(row == 0, jnp.broadcast_to(low, x.shape), pltpu.roll(x, 1, 0))
    down = jnp.where(row == count - 1, jnp.broadcast_to(high, x.shape), pltpu.roll(x, count - 1, 0))
    return up + down


def weights_of():
    center = 1.0 + 6.0 * radius_sq
    spread = relax * radius_sq / center
    scale = relax / center
    own = 1.0 - relax
    return own * (own + scale) + scale, own * spread + spread * (own + scale), spread * spread


PAD = 8


def neighbours(ref, at, inner):
    before, after = inner.start, inner.stop
    return (
        along_z(ref[at, inner, :])
        + (ref[at, before - 1 : after - 1, :] + ref[at, before + 1 : after + 1, :])
        + (ref[at - 1, inner, :] + ref[at + 1, inner, :])
    )


def step_planes(width_x):
    planes = 8
    while width_x % planes:
        planes //= 2
    return planes


def scatter_kernel(inside_ref, given_ref, index_ref, field_at, out_at, face_ref, xs_ref, ys_ref, val_ref, y_ref, field_ref, wide_ref, near_ref, out_ref, sems, *, capacity):
    rows = val_ref.shape[0]
    width_x, width_y = ys_ref.shape[0], xs_ref.shape[1]
    depth = out_ref.shape[2]
    inner = slice(PAD, PAD + width_y)
    _, ceiling = constants()
    inverse = 1.0 / ceiling
    once, near, far = weights_of()
    planes = step_planes(width_x)
    tile = planes * width_y
    steps = width_x // planes
    lead = 2 * planes + 3

    def load(i):
        at = pl.ds(pl.multiple_of(i * tile, tile), tile)
        return pltpu.make_async_copy(field_at.at[at], field_ref.at[at], sems.at[steps + i])

    for i in range(steps):
        load(i).start()
    stride = given_ref.shape[0] * capacity // rows
    for d in range(rows // capacity):
        at = slice(d * capacity, (d + 1) * capacity)
        high, low = parts(given_ref[d * stride : d * stride + capacity, :], 2)
        val_ref[at, :depth] = high
        val_ref[at, depth:] = low
    joint = index_ref[...]
    y_row = jnp.broadcast_to(joint % width_y, (width_y, rows))
    y_ref[...] = (lax.broadcasted_iota(I32, (width_y, rows), 0) == y_row).astype(F32).astype(BF16)
    x_row = joint // width_y
    for ref in (wide_ref, near_ref):
        edges = (*range(lead), lead + width_x)
        for x in edges:
            ref[x] = jnp.zeros(ref.shape[1:], F32)
        ref[lead : lead + width_x, 0:PAD, :] = jnp.zeros((width_x, PAD, depth), F32)
        ref[lead : lead + width_x, PAD + width_y :, :] = jnp.zeros((width_x, PAD, depth), F32)
    def sums(x):
        near_ref[x, inner, :] = neighbours(wide_ref, x, inner)

    def sweeps(x):
        out_ref[x] = (
            once * wide_ref[x, inner, :]
            + near * near_ref[x, inner, :]
            + far * neighbours(near_ref, x, inner)
        )

    def store(i):
        at = i * planes
        return pltpu.make_async_copy(
            out_ref.at[pl.ds(lead + at, planes)], out_at.at[pl.ds(at, planes)], sems.at[i]
        )

    def gather(i):
        at = i * planes
        here = []
        for j in range(planes):
            at_x = (x_row == at + j).astype(F32)
            here.append(y_ref[...] * jnp.broadcast_to(at_x, (width_y, rows)).astype(BF16))
        summed = dot_nn(jnp.concatenate(here, axis=0), val_ref[...])
        return summed[:, :depth] + summed[:, depth:]

    def spread(i, summed):
        field = field_ref[pl.ds(pl.multiple_of(i * tile, tile), tile), :]
        source = summed * slope_of(field, inverse)
        wide_ref[pl.ds(lead + i * planes, planes), inner, :] = source.reshape(planes, width_y, depth)

    def step(i, _):
        load(i).wait()
        at = i * planes
        for j in range(planes):
            sweeps(lead + at - 2 * planes - 2 + j)
        for j in range(planes):
            sums(lead + at - planes - 1 + j)
        near_ref[lead - 1, inner, :] = jnp.zeros((width_y, depth), F32)
        spread(i, gather(i))

        def done():
            store(i - 3).start()

        pl.when(i >= 3)(done)
        return 0

    summed = gather(0)
    load(0).wait()
    spread(0, summed)
    lax.fori_loop(1, steps, step, 0)
    for x in range((steps - 1) * planes - 1, width_x):
        sums(lead + x)
    for x in range((steps - 2) * planes - 2, width_x):
        sweeps(lead + x)
    for i in range(max(0, steps - 3), steps):
        store(i).start()
    for k, x in enumerate((0, 1, width_x - 2, width_x - 1)):
        face_ref[k] = wide_ref[lead + x, inner, :]
        xs_ref[k] = out_ref[lead + x]
    xs_ref[0] = xs_ref[0] + (far * inside_ref[0]) * face_ref[0]
    xs_ref[3] = xs_ref[3] + (far * inside_ref[1]) * face_ref[3]
    block = slice(lead, lead + width_x)
    ys_ref[:, 0:PAD, :] = out_ref[block, 0:PAD, :]
    ys_ref[:, PAD : 2 * PAD, :] = out_ref[block, width_y - PAD :, :]
    for y, at, side in ((0, 0, 2), (width_y - 1, 2 * PAD - 1, 3)):
        add = (far * inside_ref[side]) * wide_ref[block, PAD + y, :]
        ys_ref[:, at, :] = ys_ref[:, at, :] + add
        for k, x in enumerate((0, 1, width_x - 2, width_x - 1)):
            row = slice(y, y + 1)
            xs_ref[k, row, :] = xs_ref[k, row, :] + add[x : x + 1]
    for i in range(steps):
        store(i).wait()


def border_kernel(inside_ref, odd_ref, partial_at, xs_ref, ys_ref, xeven_ref, xodd_ref, yeven_ref, yodd_ref, out_at, xwork_ref, ywork_ref, sems):
    width_x, _, depth = ys_ref.shape
    width_y = xs_ref.shape[1]
    _, near, far = weights_of()

    def pick(odd, even, other):
        return jnp.where(odd, even, other), jnp.where(odd, other, even)

    xodd, yodd = odd_ref[0] == 1, odd_ref[1] == 1
    xlow, xhigh = pick(xodd, xeven_ref[...], xodd_ref[...])
    ylow, yhigh = pick(yodd, yeven_ref[...], yodd_ref[...])
    low_corners = xlow[2 * width_y : 2 * width_y + 2]
    high_corners = xhigh[2 * width_y : 2 * width_y + 2]

    def layer(halo, beyond, inside, low, high):
        ring = inside * (along_z(halo) + along_rows(halo, low, high) + beyond)
        return near * halo + far * (along_z(halo) + along_rows(halo) + ring), far * halo

    def two(layers, width):
        return layers[:width], layers[width : 2 * width]

    beyond, halo = two(xlow, width_y)
    xlow = layer(halo, beyond, inside_ref[0], low_corners[0:1], low_corners[1:2])
    halo, beyond = two(xhigh, width_y)
    xhigh = layer(halo, beyond, inside_ref[1], high_corners[0:1], high_corners[1:2])
    ylow = layer(ylow[1], ylow[0], inside_ref[2], low_corners[0:1], high_corners[0:1])
    yhigh = layer(yhigh[0], yhigh[1], inside_ref[3], low_corners[1:2], high_corners[1:2])
    ywork_ref[...] = ys_ref[...]
    for y, add in ((0, ylow[0]), (1, ylow[1]), (2 * PAD - 2, yhigh[1]), (2 * PAD - 1, yhigh[0])):
        ywork_ref[:, y, :] = ywork_ref[:, y, :] + add
    for k, (x, add) in enumerate(((0, xlow[0]), (1, xlow[1]), (width_x - 2, xhigh[1]), (width_x - 1, xhigh[0]))):
        xwork_ref[k] = xs_ref[k] + add
        for y, more in ((0, ylow[0]), (1, ylow[1]), (width_y - 2, yhigh[1]), (width_y - 1, yhigh[0])):
            row = slice(y, y + 1)
            xwork_ref[k, row, :] = xwork_ref[k, row, :] + more[x : x + 1]
    middle = pl.ds(2, width_x - 4)
    stores = [
        (xwork_ref.at[pl.ds(0, 2)], out_at.at[pl.ds(0, 2)]),
        (xwork_ref.at[pl.ds(2, 2)], out_at.at[pl.ds(width_x - 2, 2)]),
        (ywork_ref.at[middle, pl.ds(0, PAD)], out_at.at[middle, pl.ds(0, PAD)]),
        (ywork_ref.at[middle, pl.ds(PAD, PAD)], out_at.at[middle, pl.ds(width_y - PAD, PAD)]),
    ]
    for store in fetch([a for a, _ in stores], [b for _, b in stores], sems):
        store.wait()


def reply_kernel(rank_ref, owner_ref, reply_ref, out_ref):
    devices, capacity = reply_ref.shape
    count = rank_ref.shape[1]
    at_rank = (lax.broadcasted_iota(I32, (capacity, count), 0) == rank_ref[...]).astype(F32).astype(BF16)
    total = jnp.zeros((devices, count), F32)
    for piece in parts(reply_ref[...], 3):
        total = total + dot_nn(piece, at_rank)
    match = lax.broadcasted_iota(I32, (devices, count), 0) == owner_ref[...]
    out_ref[...] = jnp.sum(jnp.where(match, total, 0.0), axis=0, keepdims=True)


def swap(x, axis, odd):
    count = lax.axis_size(axis)
    pairs = [(i, i + 1) for i in range(odd, count - 1, 2)]
    return lax.ppermute(x, axis, pairs + [(j, i) for i, j in pairs])


def body(velocity, adjoint, coupling, jac_weight, owner, local_block, offsets, margin, filtered):
    both = ("brick", "dom")
    brick_count = lax.axis_size("brick")
    dom_count = lax.axis_size("dom")
    devices = brick_count * dom_count
    count = owner.shape[0]
    width_x, width_y, depth = filtered.shape
    capacity = max(2, 2 * count // devices)
    slots = devices * capacity
    shape = jax.ShapeDtypeStruct
    vmem = pl.BlockSpec(memory_space=pltpu.VMEM)
    smem = pl.BlockSpec(memory_space=pltpu.SMEM)
    hbm = pl.BlockSpec(memory_space=pltpu.HBM)

    brick, dom = lax.axis_index("brick"), lax.axis_index("dom")
    inside = jnp.stack([brick > 0, brick < brick_count - 1, dom > 0, dom < dom_count - 1]).astype(F32)
    odd = jnp.stack([brick % 2, dom % 2]).astype(I32)
    owner_row = owner.reshape(1, count)
    stride = capacity + -(-2 * capacity // depth)
    lanes = 128
    turned = (count // lanes, lanes, offsets.shape[0])
    outgoing, rank = pl.pallas_call(
        functools.partial(send_kernel, devices=devices, capacity=capacity),
        out_shape=(shape((devices * stride, depth), F32), shape((1, count), I32)),
        in_specs=[hbm] * 8,
        out_specs=(vmem, vmem),
        scratch_shapes=[
            pltpu.VMEM((1, count), I32),
            pltpu.VMEM((1, count), I32),
            pltpu.VMEM((1, count), F32),
            pltpu.VMEM(velocity.shape, BF16),
            pltpu.VMEM(adjoint.shape, BF16),
            pltpu.VMEM(coupling.shape, BF16),
            pltpu.VMEM(offsets.shape, I32),
            pltpu.VMEM(margin.shape, F32),
            pltpu.VMEM(turned, I32),
            pltpu.VMEM(turned, I32),
            pltpu.VMEM(turned, F32),
            pltpu.VMEM(turned, F32),
            pltpu.VMEM((count * depth // lanes, lanes), F32),
            pltpu.VMEM((2 * depth, count), BF16),
            pltpu.SemaphoreType.DMA((8,)),
        ],
        compiler_params=params(VMEM_WHOLE),
        name="send",
    )(
        owner_row,
        local_block.reshape(1, count),
        jac_weight.reshape(1, count),
        velocity,
        adjoint,
        coupling,
        offsets,
        margin,
    )
    got = lax.all_to_all(
        outgoing.reshape(devices, 1, stride * depth), both, split_axis=0, concat_axis=0, tiled=True
    ).reshape(devices * stride, depth)
    field = filtered.reshape(width_x * width_y, depth)
    face_y = shape((2, width_x, depth), F32)
    values, index, yeven, yodd, density = pl.pallas_call(
        functools.partial(owner_kernel, capacity=capacity, width_y=width_y),
        out_shape=(
            shape(got.shape, F32),
            shape((1, slots), I32),
            face_y,
            face_y,
            shape((devices, 1, capacity), F32),
        ),
        in_specs=[smem, smem, vmem, vmem],
        out_specs=(vmem,) * 5,
        input_output_aliases={2: 0},
        scratch_shapes=[
            pltpu.VMEM((devices, depth), F32),
            pltpu.VMEM((devices, depth), I32),
            pltpu.VMEM((slots, depth), F32),
            pltpu.VMEM((slots, 2 * depth), BF16),
            pltpu.VMEM((4 * width_x, slots), BF16),
        ],
        compiler_params=params(),
        name="owners",
    )(odd, got[capacity::stride].astype(I32), got, field)
    planes_x = width_x + 2 * step_planes(width_x) + 4
    wide = pltpu.VMEM((planes_x, width_y + 2 * PAD, depth), F32)
    partial, face, xs, ys = pl.pallas_call(
        functools.partial(scatter_kernel, capacity=capacity),
        out_shape=(
            shape(filtered.shape, F32),
            shape((4, width_y, depth), F32),
            shape((4, width_y, depth), F32),
            shape((width_x, 2 * PAD, depth), F32),
        ),
        in_specs=[smem, vmem, vmem, hbm],
        out_specs=(hbm, vmem, vmem, vmem),
        scratch_shapes=[
            pltpu.VMEM((slots, 2 * depth), BF16),
            pltpu.VMEM((width_y, slots), BF16),
            pltpu.VMEM(field.shape, F32),
            wide,
            wide,
            pltpu.VMEM((planes_x, width_y, depth), F32),
            pltpu.SemaphoreType.DMA((2 * width_x // step_planes(width_x),)),
        ],
        compiler_params=params(),
        cost_estimate=pl.CostEstimate(
            flops=8 * slots * field.size, bytes_accessed=16 * field.size, transcendentals=field.size
        ),
        name="scatter",
    )(inside, values, index, pltpu.with_memory_space_constraint(field, pltpu.HBM))

    reply = lax.all_to_all(
        density, both, split_axis=0, concat_axis=0, tiled=True
    )
    yeven, yodd = swap(yeven, "dom", 0), swap(yodd, "dom", 1)
    dom_odd, brick_odd = dom % 2 == 1, brick % 2 == 1
    ylow, yhigh = jnp.where(dom_odd, yeven, yodd), jnp.where(dom_odd, yodd, yeven)
    filler = jnp.zeros((6, depth), F32)
    top = jnp.concatenate([face[2], face[3], ylow[1, width_x - 1 :], yhigh[0, width_x - 1 :], filler])
    bottom = jnp.concatenate([face[0], face[1], ylow[1, :1], yhigh[0, :1], filler])
    top, bottom, reply = lax.optimization_barrier((top, bottom, reply))
    xeven = swap(jnp.where(brick_odd, bottom, top), "brick", 0)
    xodd = swap(jnp.where(brick_odd, top, bottom), "brick", 1)
    element_density = pl.pallas_call(
        reply_kernel,
        out_shape=shape((1, count), F32),
        compiler_params=params(),
        name="reply",
    )(rank, owner_row, reply.reshape(devices, capacity))

    result = pl.pallas_call(
        border_kernel,
        out_shape=shape(filtered.shape, F32),
        in_specs=[smem, smem, hbm] + [vmem] * 6,
        out_specs=hbm,
        scratch_shapes=[pltpu.VMEM(xs.shape, F32), pltpu.VMEM(ys.shape, F32), pltpu.SemaphoreType.DMA((4,))],
        input_output_aliases={2: 0},
        compiler_params=params(),
        name="border",
    )(inside, odd, partial, xs, ys, xeven, xodd, yeven, yodd)
    return (result, element_density.reshape(count))


def solution(mesh):
    return jax.shard_map(
        body,
        mesh=mesh,
        in_specs=(
            P(None, None, ("brick", "dom")),
            P(None, None, ("brick", "dom")),
            P(),
            P(("brick", "dom")),
            P(("brick", "dom"), None),
            P(("brick", "dom")),
            P(None, ("brick", "dom")),
            P(None, ("brick", "dom")),
            P("brick", "dom", None),
        ),
        out_specs=(P("brick", "dom", None), P(("brick", "dom"))),
        check_vma=False,
    )
```
